256 devices in a mesh: gx: 8 (over x, core), gy: 32 (over y, z).
Axes of the slice: x: 4, y: 4, z: 8, core: 2. Of those that a mesh axis runs over, the one named last changes fastest.
Arguments:
- velocity: float32 [2, 11, 64, 4096], P(None, None, 'gx', 'gy'), may hold values from -6 to 6
- thickness: float32 [64, 4096], P('gx', 'gy'), may hold values from 0.5 to 2
- log_friction: float32 [64, 4096], P('gx', 'gy'), may hold values from -1 to 1
- obs_weight: float32 [64, 4096], P('gx', 'gy'), may hold values from 0.5 to 4
- ice_mask: int32 [64, 4096], P('gx', 'gy'), may hold values 0 or 1
- grounded: int32 [64, 4096], P('gx', 'gy'), may hold values 0 or 1
- probes: float32 [8, 64, 4096], P(None, 'gx', 'gy'), may hold values from -6 to 6
Outputs:
- hess_probe: float32 [8, 64, 4096], P(None, 'gx', 'gy')
The draws below stay inside these ranges and needn't reach their ends.
All inputs are finite; a program needn't handle non-finite values. No bound on the sum of `ice_mask` or of `grounded` on one device may be relied on, other than what follows from the above.
Results may differ from the reference program's by a relative error of at most 0.0003.
Values sent between devices are 32-bit elements; how exact they have to be, the bound alone decides.
No kernel may reach another device: no remote copies, remote signals or barrier semaphores. Data moves between devices by JAX's collectives and lax.ppermute only.
A program may use at most 64 MiB of HBM per device.

```python
import math
import jax
import jax.numpy as jnp
from jax import lax

NL = 11
PROBES = 8
NX = 64
NY = 4096


def set_ends(values, key, least, largest):
    longest = values.shape.index(max(values.shape))
    spots = []
    for shift in (0, 1):
        where = [jax.random.randint(jax.random.fold_in(key, axis), (), 0, length) for axis, length in enumerate(values.shape)]
        where[longest] = (where[longest] + shift) % values.shape[longest]
        spots.append(tuple(where))
    return values.at[spots[0]].set(least).at[spots[1]].set(largest)


def level_of(rng, shape, shards, least, largest):
    loudness, own = 1.0, jax.random.fold_in(rng, 6)
    for dim, blocks in shards:
        steps = jnp.exp(jax.random.uniform(jax.random.fold_in(own, dim), (blocks,), jnp.float32, least / len(shards), largest / len(shards)))
        loudness = loudness * jnp.repeat(steps, shape[dim] // blocks).reshape([-1 if axis == dim else 1 for axis in range(len(shape))])
    return loudness


def centred(stream_key, dims, scale, limit, split=(), kind=jnp.bfloat16):
    drawn = jax.random.normal(stream_key, dims, jnp.float32) * scale
    if len(split) > 0:
        drawn = level_of(stream_key, dims, split, -0.22, 0.18) * drawn
    return jnp.clip(drawn, min=-limit, max=limit).astype(kind)


def setup_inputs(seed: int = 0) -> dict:
    key_list = jax.random.split(jax.random.key(seed), 8)
    return {
        "velocity": centred(key_list[0], (2, NL, NX, NY), 1.0, 6.0, ((2, 8), (3, 32)), jnp.float32),
        "thickness": jnp.clip(0.5 + 1.5 * jax.random.uniform(key_list[1], (NX, NY), jnp.float32) ** level_of(key_list[1], (NX, NY), ((0, 8), (1, 32)), -0.2, 0.2), 0.5, 2.0),
        "log_friction": jnp.clip(jax.random.uniform(key_list[2], (NX, NY), jnp.float32, -1.0, 1.0) * level_of(key_list[2], (NX, NY), ((0, 8), (1, 32)), -0.4, 0.0), -1.0, 1.0),
        "obs_weight": jnp.clip(jnp.exp(math.log(4.0) - 2.0794415 * jax.random.uniform(key_list[3], (NX, NY), jnp.float32) ** level_of(key_list[3], (NX, NY), ((0, 8), (1, 32)), -0.2, 0.2)), 0.5, 4.0),
        "ice_mask": set_ends((jax.random.randint(key_list[4], (NX, NY), 0, 4) < 3).astype(jnp.int32), jax.random.fold_in(key_list[4], 1), 0, 1),
        "grounded": set_ends((jax.random.randint(key_list[5], (NX, NY), 0, 3) < 2).astype(jnp.int32), jax.random.fold_in(key_list[5], 1), 0, 1),
        "probes": centred(key_list[6], (PROBES, NX, NY), 1.0, 6.0, ((1, 8), (2, 32)), jnp.float32),
    }


PRECISE = lax.Precision.HIGHEST
MASS_TERM = 0.1
STRAIN_OFFSET = 0.01

def viscosity(velocity_ext, thick_ext):
    layers = velocity_ext.shape[1]
    step_z = thick_ext[1:-1, 1:-1] / (layers - 1)
    speed_u = velocity_ext[0]
    speed_v = velocity_ext[1]
    grad_ux = 0.5 * (speed_u[:, 2:, 1:-1] - speed_u[:, :-2, 1:-1])
    grad_uy = 0.5 * (speed_u[:, 1:-1, 2:] - speed_u[:, 1:-1, :-2])
    grad_vx = 0.5 * (speed_v[:, 2:, 1:-1] - speed_v[:, :-2, 1:-1])
    grad_vy = 0.5 * (speed_v[:, 1:-1, 2:] - speed_v[:, 1:-1, :-2])
    middle = velocity_ext[:, :, 1:-1, 1:-1]
    column = jnp.concatenate([middle[:, :1], middle, middle[:, -1:]], axis=1)
    vertical_grad = (column[:, 2:] - column[:, :-2]) / (2.0 * step_z)
    strain = grad_ux * grad_ux + grad_vy * grad_vy + grad_ux * grad_vy + 0.25 * (grad_uy + grad_vx) ** 2 + 0.25 * (vertical_grad[0] ** 2 + vertical_grad[1] ** 2) + STRAIN_OFFSET
    return 0.5 * strain ** (-1.0 / 3.0)

def coefficients(visc_ext, mask_ext, thickness, grounded_f, log_friction):
    layers = visc_ext.shape[0]
    coef_x = 0.5 * (visc_ext[:, :-1, 1:-1] + visc_ext[:, 1:, 1:-1]) * (mask_ext[:-1, 1:-1] * mask_ext[1:, 1:-1])
    coef_y = 0.5 * (visc_ext[:, 1:-1, :-1] + visc_ext[:, 1:-1, 1:]) * (mask_ext[1:-1, :-1] * mask_ext[1:-1, 1:])
    interior = visc_ext[:, 1:-1, 1:-1]
    inverse_step = (layers - 1) / thickness
    coef_z = 0.5 * (interior[:-1] + interior[1:]) * (inverse_step * inverse_step)
    ice_own = mask_ext[1:-1, 1:-1]
    friction = ice_own * grounded_f * jnp.exp(log_friction)
    diag_base = MASS_TERM * ice_own + (1.0 - ice_own)
    zeros_upper = jnp.zeros((layers - 1,) + diag_base.shape, jnp.float32)
    diagonal = diag_base[None] + jnp.concatenate([friction[None], zeros_upper], axis=0)
    return (coef_x, coef_y, coef_z, diagonal, friction)

def anisotropy():
    aniso_x = jnp.array([4.0, 1.0], jnp.float32).reshape(2, 1, 1, 1)
    aniso_y = jnp.array([1.0, 4.0], jnp.float32).reshape(2, 1, 1, 1)
    return (aniso_x, aniso_y)

def operator_apply(extended, coef_x, coef_y, coef_z, diagonal):
    aniso_x, aniso_y = anisotropy()
    interior = extended[..., 1:-1, 1:-1]
    flux_x = coef_x * (extended[..., 1:, 1:-1] - extended[..., :-1, 1:-1])
    flux_y = coef_y * (extended[..., 1:-1, 1:] - extended[..., 1:-1, :-1])
    flux_z = coef_z * (interior[..., 1:, :, :] - interior[..., :-1, :, :])
    boundary_zero = jnp.zeros_like(flux_z[..., :1, :, :])
    vertical = jnp.concatenate([boundary_zero, flux_z], axis=-3) - jnp.concatenate([flux_z, boundary_zero], axis=-3)
    horizontal = aniso_x * (flux_x[..., :-1, :] - flux_x[..., 1:, :]) + aniso_y * (flux_y[..., :-1] - flux_y[..., 1:])
    return horizontal + vertical + diagonal * interior

def column_factors(coef_x, coef_y, coef_z, diagonal):
    aniso_x, aniso_y = anisotropy()
    layers = diagonal.shape[0]
    lateral = aniso_x * (coef_x[:, :-1] + coef_x[:, 1:]) + aniso_y * (coef_y[:, :, :-1] + coef_y[:, :, 1:])
    zero_layer = jnp.zeros_like(coef_z[:1])
    main_diag = lateral + diagonal + jnp.concatenate([zero_layer, coef_z], axis=0) + jnp.concatenate([coef_z, zero_layer], axis=0)
    ratios = []
    inverses = []
    for layer_index in range(layers):
        pivot_value = main_diag[:, layer_index]
        if layer_index > 0:
            pivot_value = pivot_value - coef_z[layer_index - 1] * ratios[-1]
        inverse = 1.0 / pivot_value
        inverses.append(inverse)
        if layer_index < layers - 1:
            ratios.append(coef_z[layer_index] * inverse)
    return (jnp.stack(ratios, axis=1), jnp.stack(inverses, axis=1))

def column_solve(residual, coef_z, ratios, inverses):
    layers = residual.shape[-3]
    forward_pass = []
    for layer_index in range(layers):
        current = residual[..., layer_index, :, :]
        if layer_index > 0:
            current = current + coef_z[layer_index - 1] * forward_pass[-1]
        forward_pass.append(current * inverses[:, layer_index])
    result = [forward_pass[-1]]
    for layer_index in range(layers - 2, -1, -1):
        result.append(forward_pass[layer_index] + ratios[:, layer_index] * result[-1])
    return jnp.stack(result[::-1], axis=-3)

def gram_matrix(left_block, right_block):
    probe_count = left_block.shape[0]
    return lax.dot_general(left_block.reshape(probe_count, -1), right_block.reshape(probe_count, -1), (((1,), (1,)), ((), ())), precision=PRECISE)

def combine(vectors, mixing):
    return jnp.tensordot(mixing, vectors, axes=((0,), (0,)), precision=PRECISE)

def small_solve(matrix, right_side):
    factor = jnp.linalg.cholesky(matrix)
    return jax.scipy.linalg.cho_solve((factor, True), right_side)

def block_solve(right_side, apply_fn, precond_fn):
    residual = right_side
    search = precond_fn(residual)
    norm_old = gram_matrix(residual, search)
    image = apply_fn(search)
    curvature = gram_matrix(search, image)
    step_mix = small_solve(curvature, norm_old)
    solution = combine(search, step_mix)
    residual = residual - combine(image, step_mix)
    precon = precond_fn(residual)
    norm_new = gram_matrix(residual, precon)
    update_mix = small_solve(norm_old, norm_new)
    search = precon + combine(search, update_mix)
    image = apply_fn(search)
    curvature = gram_matrix(search, image)
    step_mix = small_solve(curvature, norm_new)
    return solution + combine(search, step_mix)

def reference(velocity, thickness, log_friction, obs_weight, ice_mask, grounded, probes):
    layers = velocity.shape[1]
    mask_f = ice_mask.astype(jnp.float32)
    grounded_f = grounded.astype(jnp.float32)
    velocity_ext = jnp.pad(velocity, ((0, 0), (0, 0), (1, 1), (1, 1)))
    thick_ext = jnp.pad(thickness, 1, mode='edge')
    visc_node = viscosity(velocity_ext, thick_ext)
    visc_ext = jnp.pad(jnp.where(mask_f[None] > 0.5, visc_node, 0.0), ((0, 0), (1, 1), (1, 1)))
    mask_ext = jnp.pad(mask_f, 1)
    coef_x, coef_y, coef_z, diagonal, friction = coefficients(visc_ext, mask_ext, thickness, grounded_f, log_friction)
    ratios, inverses = column_factors(coef_x, coef_y, coef_z, diagonal)

    def apply_one(single):
        return operator_apply(jnp.pad(single, ((0, 0), (0, 0), (1, 1), (1, 1))), coef_x, coef_y, coef_z, diagonal)

    def apply_all(vectors):
        return lax.map(apply_one, vectors)

    def precond_all(vectors):
        return lax.map(lambda single: column_solve(single, coef_z, ratios, inverses), vectors)
    probe_count = probes.shape[0]
    upper_zero = jnp.zeros((probe_count, 2, layers - 1) + thickness.shape, jnp.float32)
    bottom = (friction[None] * probes)[:, None] * velocity[None, :, 0]
    forward_rhs = jnp.concatenate([bottom[:, :, None], upper_zero], axis=2)
    delta_u = block_solve(forward_rhs, apply_all, precond_all)
    surface = (obs_weight * mask_f)[None, None] * delta_u[:, :, layers - 1]
    adjoint_rhs = jnp.concatenate([upper_zero, surface[:, :, None]], axis=2)
    delta_lam = block_solve(adjoint_rhs, apply_all, precond_all)
    return friction[None] * jnp.sum(velocity[None, :, 0] * delta_lam[:, :, 0], axis=1)
```

```python
import functools

import jax
import jax.numpy as jnp
from jax import lax
from jax.experimental import pallas as pl
from jax.experimental.pallas import tpu as pltpu
from jax.sharding import PartitionSpec as P

MASS_TERM = 0.1
STRAIN_OFFSET = 0.01
PRECISE = lax.Precision.HIGHEST

ROWS = 16
LANES = 256
OWN_X = 8
OWN_Y = 128
LOW = 4
THICK, MASK, FRIC, OBS, PROBE = 22, 23, 24, 25, 26
PLANES = 40


def dot(left, right, dims=((1,), (0,))):
    return lax.dot_general(
        left, right, (dims, ((), ())), precision=PRECISE, preferred_element_type=jnp.float32
    )


def shift(plane, step, axis):
    size = plane.shape[axis]
    return pltpu.roll(plane, (-step) % size, axis)


def pack_kernel(vel, thick, logf, obs, mask, ground, probes, own, up, down):
    m = mask[...].astype(jnp.float32)
    fric = m * ground[...].astype(jnp.float32) * jnp.exp(logf[...])
    fields = [vel[c, l] for c in range(2) for l in range(11)]
    fields += [thick[...], m, fric, obs[...] * m]
    fields += [probes[a] for a in range(8)]
    for k, field in enumerate(fields):
        own[k] = field
        up[pl.ds(LOW * k, LOW), :] = field[OWN_X - LOW :]
        down[pl.ds(LOW * k, LOW), :] = field[:LOW]
        if k < 22:
            down[pl.ds(LOW * PLANES + k, 1), :] = field[LOW : LOW + 1]


def strip_kernel(edge, own, low, high, tall, left, right):
    keep_low = jnp.where(edge[0] == 0, 0.0, 1.0)
    keep_high = jnp.where(edge[1] == 0, 0.0, 1.0)
    for k in range(34):
        tall[k, 0:OWN_X, :] = own[k]
        tall[k, OWN_X : OWN_X + LOW, :] = high[pl.ds(LOW * k, LOW), :] * keep_high
        tall[k, ROWS - LOW : ROWS, :] = low[pl.ds(LOW * k, LOW), :] * keep_low
    for k in range(34, PLANES):
        tall[k] = jnp.zeros((ROWS, OWN_Y), jnp.float32)
    for b in range(PLANES // 8):
        turned = tall[8 * b : 8 * b + 8].reshape(8 * ROWS, OWN_Y).T
        left[:, OWN_Y * b : OWN_Y * (b + 1)] = turned[0:8]
        right[:, OWN_Y * b : OWN_Y * (b + 1)] = turned[OWN_Y - 8 : OWN_Y]


def moments_kernel(
    edge, tall, high, from_left, from_right, gram, mixes,
    full, row12, mu, kx, kxm, ky, kym, kz, inv, ratio, resp, phi, gam, wts, basis, lhs, rhs,
):
    keep_left = jnp.where(edge[2] == 0, 0.0, 1.0)
    keep_right = jnp.where(edge[3] == 0, 0.0, 1.0)
    keep_high = jnp.where(edge[1] == 0, 0.0, 1.0)
    gap = jnp.zeros((OWN_Y - 16, OWN_Y), jnp.float32)
    for b in range(PLANES // 8):
        cols = slice(OWN_Y * b, OWN_Y * (b + 1))
        block = jnp.concatenate(
            [from_right[:, cols] * keep_right, gap, from_left[:, cols] * keep_left], axis=0
        )
        full[8 * b : 8 * b + 8, :, OWN_Y:] = block.T.reshape(8, ROWS, OWN_Y)
        full[8 * b : 8 * b + 8, :, :OWN_Y] = tall[8 * b : 8 * b + 8]
    row12[...] = high[pl.ds(LOW * PLANES, 24), :] * keep_high

    m = full[MASK]
    icy = m > 0.5
    thick = jnp.where(icy, full[THICK], 1.0)
    steep = 10.0 / thick
    half_steep = 0.5 * steep
    steep2 = 0.5 * steep * steep
    mm_x = 0.5 * (m * shift(m, 1, 0))
    mm_y = 0.5 * (m * shift(m, 1, 1))
    fric = full[FRIC]
    base = MASS_TERM * m + (1.0 - m)
    last = lax.broadcasted_iota(jnp.int32, (ROWS, LANES), 0) == OWN_X + LOW - 1

    for l in range(11):
        grads = []
        for c in range(2):
            w = full[11 * c + l]
            beyond = jnp.concatenate(
                [row12[11 * c + l : 11 * c + l + 1, :], jnp.zeros((1, OWN_Y), jnp.float32)], axis=1
            )
            ahead = jnp.where(last, jnp.broadcast_to(beyond, (ROWS, LANES)), shift(w, 1, 0))
            gx = 0.5 * (ahead - shift(w, -1, 0))
            gy = 0.5 * (shift(w, 1, 1) - shift(w, -1, 1))
            gz = (full[11 * c + min(l + 1, 10)] - full[11 * c + max(l - 1, 0)]) * half_steep
            grads.append((gx, gy, gz))
        (ux, uy, uz), (vx, vy, vz) = grads
        cross = uy + vx
        e2 = ux * ux + vy * vy + ux * vy + 0.25 * (cross * cross + uz * uz + vz * vz) + STRAIN_OFFSET
        mu[l] = jnp.where(icy, 0.5 * jnp.exp(jnp.log(e2) * (-1.0 / 3.0)), 0.0)

    kz[0] = jnp.zeros((ROWS, LANES), jnp.float32)
    kz[11] = jnp.zeros((ROWS, LANES), jnp.float32)
    for l in range(11):
        here = mu[l]
        ex = (here + shift(here, 1, 0)) * mm_x
        ey = (here + shift(here, 1, 1)) * mm_y
        kx[l] = ex
        ky[l] = ey
        kxm[l] = shift(ex, -1, 0)
        kym[l] = shift(ey, -1, 1)
        if l < 10:
            kz[l + 1] = (here + mu[l + 1]) * steep2

    for c in range(2):
        a, b = (4.0, 1.0) if c == 0 else (1.0, 4.0)
        source = fric * full[11 * c]
        last_ratio = None
        carry = None
        for l in range(11):
            main = a * (kx[l] + kxm[l]) + b * (ky[l] + kym[l]) + base + kz[l] + kz[l + 1]
            if l == 0:
                main = main + fric
            else:
                main = main - kz[l] * last_ratio
            recip = 1.0 / main
            last_ratio = kz[l + 1] * recip
            inv[c, l] = recip
            ratio[c, l] = last_ratio
            carry = (source if l == 0 else kz[l] * carry) * recip
            resp[c, l] = carry
        top = inv[c, 10]
        resp[2 + c, 10] = top
        for l in range(9, -1, -1):
            step = ratio[c, l]
            carry = resp[c, l] + step * carry
            resp[c, l] = carry
            top = step * top
            resp[2 + c, l] = top

    def one_kind(kc, _):
        c = lax.rem(kc, 2)
        a = jnp.where(c == 0, 4.0, 1.0)
        b = 5.0 - a
        carry = [None] * 4
        n1x = jnp.zeros((OWN_X, OWN_Y), jnp.float32)
        n1y = n1x
        for l in range(11):
            e = resp[kc, l]
            parts = [
                a * (kx[l] * shift(e, 1, 0)),
                a * (kxm[l] * shift(e, -1, 0)),
                b * (ky[l] * shift(e, 1, 1)),
                b * (kym[l] * shift(e, -1, 1)),
            ]
            scale = inv[c, l]
            for s in range(4):
                phi[s, l] = parts[s][:OWN_X, :OWN_Y]
                total = parts[s] if l == 0 else parts[s] + kz[l] * carry[s]
                carry[s] = total * scale
                gam[kc, s, l] = carry[s]
            n1x = n1x + (e * parts[0])[:OWN_X, :OWN_Y]
            n1y = n1y + (e * parts[2])[:OWN_X, :OWN_Y]
        wts[kc, 1] = n1x
        wts[kc, 2] = n1y
        for l in range(9, -1, -1):
            step = ratio[c, l]
            for s in range(4):
                carry[s] = gam[kc, s, l] + step * carry[s]
                gam[kc, s, l] = carry[s]
        own = (slice(0, OWN_X), slice(0, OWN_Y))
        acc = [None] * 16
        for l in range(11):
            f = [phi[s, l] for s in range(4)]
            g = [gam[kc, s, l][own] for s in range(4)]
            for s in range(4):
                for t in range(s, 4):
                    term = f[s] * g[t]
                    acc[4 * s + t] = term if l == 0 else acc[4 * s + t] + term
        for s in range(4):
            for t in range(4):
                wts[kc, 3 + 4 * s + t] = acc[4 * min(s, t) + max(s, t)]
        for way in range(2):
            acc = [None] * 16
            for l in range(11):
                edge_k = kx[l][own] * a if way == 0 else ky[l][own] * b
                g = [gam[kc, s, l][own] * edge_k for s in range(4)]
                if way == 0:
                    h = [shift(gam[kc, s, l, :, :OWN_Y], 1, 0)[:OWN_X] for s in range(4)]
                else:
                    h = [shift(gam[kc, s, l, :OWN_X, :], 1, 1)[:, :OWN_Y] for s in range(4)]
                for s in range(4):
                    for t in range(4):
                        term = g[s] * h[t]
                        acc[4 * s + t] = term if l == 0 else acc[4 * s + t] + term
            for s in range(16):
                wts[kc, 19 + 16 * way + s] = acc[s]
        return 0

    lax.fori_loop(0, 4, one_kind, 0)
    own = (slice(0, OWN_X), slice(0, OWN_Y))
    for c in range(2):
        source = (fric * full[11 * c])[own]
        wts[c, 0] = source * resp[c, 0][own]
        wts[2 + c, 0] = resp[2 + c, 10][own]
    for k in range(51):
        wts[0, k] = wts[0, k] + wts[1, k]

    obs = full[OBS]

    def one_probe(a, _):
        p = full[PROBE + a]
        near = [shift(p, 1, 0), shift(p, -1, 0), shift(p, 1, 1), shift(p, -1, 1)]
        for c in range(2):
            basis[c, a] = obs * resp[c, 10] * p
            total = gam[c, 0, 10] * near[0]
            for s in range(1, 4):
                total = total + gam[c, s, 10] * near[s]
            basis[c, 8 + a] = obs * total
        return 0

    lax.fori_loop(0, 8, one_probe, 0)

    def terms(kc, b, plane):
        mid = plane[:, :OWN_Y]
        yp = shift(plane, 1, 1)
        ym = shift(plane, -1, 1)[:, :OWN_Y]
        y2 = shift(yp[:OWN_X], 1, 1)[:, :OWN_Y]
        yp = yp[:, :OWN_Y]
        p00 = mid[:OWN_X]
        pxp, pxm, px2 = (shift(mid, d, 0)[:OWN_X] for d in (1, -1, 2))
        pyp, pxpyp, pxmyp = yp[:OWN_X], shift(yp, 1, 0)[:OWN_X], shift(yp, -1, 0)[:OWN_X]
        pym, pxpym = ym[:OWN_X], shift(ym, 1, 0)[:OWN_X]
        near = [pxp, pxm, pyp, pym]
        past_x = [px2, p00, pxpyp, pxpym]
        past_y = [pxpyp, pxmyp, y2, p00]
        return p00, near, past_x, past_y

    def fill(kc, b, plane, many):
        p00, near, past_x, past_y = terms(kc, b, plane)
        here = pl.ds(pl.multiple_of(OWN_X * b, OWN_X), OWN_X)
        there = pl.ds(pl.multiple_of(OWN_X * (many + b), OWN_X), OWN_X)
        for t in range(4):
            second = wts[kc, 3 + 4 * t] * near[0]
            for s in range(1, 4):
                second = second + wts[kc, 3 + 4 * t + s] * near[s]
            third = wts[kc, 19 + 4 * t] * past_x[0] + wts[kc, 35 + 4 * t] * past_y[0]
            for s in range(1, 4):
                third = third + wts[kc, 19 + 4 * t + s] * past_x[s]
                third = third + wts[kc, 35 + 4 * t + s] * past_y[s]
            lhs[t, here, :] = near[t]
            rhs[t, here, :] = second
            rhs[t, there, :] = third
        lhs[4, here, :] = p00
        rhs[4, here, :] = wts[kc, 0] * p00
        rhs[4, there, :] = wts[kc, 1] * near[0] + wts[kc, 2] * near[2]
        return p00, near

    def products(many):
        rows = OWN_X * many
        nt = ((1,), (1,))
        ends = dot(lhs[4, :rows, :], rhs[4, : 2 * rows, :], nt)
        sides = dot(lhs[0, :rows, :], rhs[0, : 2 * rows, :], nt)
        for t in range(1, 4):
            sides = sides + dot(lhs[t, :rows, :], rhs[t, : 2 * rows, :], nt)
        return ends, sides

    def fold(product, many):
        rows = OWN_X * many
        same = lax.broadcasted_iota(jnp.int32, (rows, 2 * rows), 0) % OWN_X == (
            lax.broadcasted_iota(jnp.int32, (rows, 2 * rows), 1) % OWN_X
        )
        kept = jnp.where(same, product, 0.0).reshape(many, OWN_X, 2 * rows)
        narrow = jnp.sum(kept, axis=1)
        pick = lax.broadcasted_iota(jnp.int32, (2 * rows, 2 * many), 0) // OWN_X == (
            lax.broadcasted_iota(jnp.int32, (2 * rows, 2 * many), 1)
        )
        return dot(narrow, jnp.where(pick, 1.0, 0.0))

    def fill_probe(b, _):
        fill(0, b, full[PROBE + b], 8)
        return 0

    lax.fori_loop(0, 8, fill_probe, 0)
    ends, sides = products(8)
    first = jnp.concatenate([fold(ends, 8), fold(sides, 8)], axis=1)

    total_ends = total_sides = None
    for c in range(2):
        weight = (fric * full[11 * c])[own]

        def fill_basis(b, _, c=c, weight=weight):
            p00, near = fill(2 + c, b, basis[c, b], 16)
            one = weight * resp[2 + c, 0, :OWN_X, :OWN_Y] * p00
            two = gam[2 + c, 0, 0, :OWN_X, :OWN_Y] * near[0]
            for s in range(1, 4):
                two = two + gam[2 + c, s, 0, :OWN_X, :OWN_Y] * near[s]
            two = weight * two
            if c == 1:
                one = one + mixes[b]
                two = two + mixes[16 + b]
            mixes[b] = one
            mixes[16 + b] = two
            return 0

        lax.fori_loop(0, 16, fill_basis, 0)
        ends, sides = products(16)
        total_ends = ends if c == 0 else total_ends + ends
        total_sides = sides if c == 0 else total_sides + sides
    second = jnp.concatenate([fold(total_ends, 16), fold(total_sides, 16)], axis=1)
    gram[:, 0:64] = second
    gram[0:8, 64:96] = first
    gram[8:16, 64:96] = jnp.zeros((8, 32), jnp.float32)
    gram[:, 96:128] = jnp.zeros((16, 32), jnp.float32)


def turned(square):
    size = square.shape[0]
    eye = lax.broadcasted_iota(jnp.int32, (size, size), 0) == lax.broadcasted_iota(
        jnp.int32, (size, size), 1
    )
    return dot(jnp.where(eye, 1.0, 0.0), square, ((1,), (1,)))


def krylov_solve(moment0, side1, moment2, side3):
    moment1 = side1 + turned(side1)
    moment3 = side3 + turned(side3)
    low = moment1 - moment2
    system = jnp.concatenate(
        [
            jnp.concatenate([moment0 - moment1, low, moment0], axis=1),
            jnp.concatenate([low, moment2 - moment3, moment1], axis=1),
        ],
        axis=0,
    )
    row = lax.broadcasted_iota(jnp.int32, (16, 24), 0)
    for k in range(16):
        scaled = system[k : k + 1, :] / system[k : k + 1, k : k + 1]
        system = jnp.where(row == k, scaled, system - system[:, k : k + 1] * scaled)
    return system[:, 16:24]


def finish_kernel(gram, mixes, out):
    first = [gram[0:8, 64 + 8 * k : 72 + 8 * k] for k in range(4)]
    mix = krylov_solve(*first)
    tn = ((0,), (0,))
    half = dot(mix, gram[:, 0:64], tn)
    second = [dot(half[:, 16 * k : 16 * k + 16], mix) for k in range(4)]
    coef = krylov_solve(*second)
    flat = jnp.concatenate([dot(coef[0:8], mix, ((0,), (1,))), dot(coef[8:16], mix, ((0,), (1,)))], axis=1)
    tall = lax.broadcasted_iota(jnp.int32, (64, 8), 0) // 8 == lax.broadcasted_iota(jnp.int32, (64, 8), 1)
    wide = lax.broadcasted_iota(jnp.int32, (32, 256), 1) // 8 == lax.broadcasted_iota(jnp.int32, (32, 256), 0)
    spread = dot(dot(jnp.where(tall, 1.0, 0.0), flat), jnp.where(wide, 1.0, 0.0))
    same = lax.broadcasted_iota(jnp.int32, (64, 256), 0) % 8 == lax.broadcasted_iota(jnp.int32, (64, 256), 1) % 8
    spread = jnp.where(same, spread, 0.0)
    out[...] = dot(spread, mixes[...].reshape(256, OWN_Y)).reshape(8, OWN_X, OWN_Y)


VMEM = pl.BlockSpec(memory_space=pltpu.VMEM)
SMEM = pl.BlockSpec(memory_space=pltpu.SMEM)


def shaped(*dims):
    return jax.ShapeDtypeStruct(dims, jnp.float32)


def spread_sum(values, axis):
    count = lax.axis_size(axis)
    copies = jnp.broadcast_to(values, (count,) + values.shape)
    return jnp.sum(lax.all_to_all(copies, axis, 0, 0), axis=0)


def ring(values, axis, step):
    count = lax.axis_size(axis)
    return lax.ppermute(values, axis, [(i, (i + step) % count) for i in range(count)])


def body(velocity, thickness, log_friction, obs_weight, ice_mask, grounded, probes):
    at_x, at_y = lax.axis_index("gx"), lax.axis_index("gy")
    edge = jnp.stack(
        [at_x, lax.axis_size("gx") - 1 - at_x, at_y, lax.axis_size("gy") - 1 - at_y]
    ).astype(jnp.int32)
    limit = pltpu.CompilerParams(vmem_limit_bytes=48 * 1024 * 1024)
    own, up, down = pl.pallas_call(
        pack_kernel,
        out_shape=(shaped(PLANES, OWN_X, OWN_Y), shaped(LOW * PLANES + 24, OWN_Y), shaped(LOW * PLANES + 24, OWN_Y)),
        in_specs=[VMEM] * 7,
        out_specs=(VMEM,) * 3,
        compiler_params=limit,
        name="pack",
    )(velocity, thickness, log_friction, obs_weight, ice_mask, grounded, probes)
    low = ring(up, "gx", 1)
    high = ring(down, "gx", -1)
    tall, left, right = pl.pallas_call(
        strip_kernel,
        out_shape=(shaped(PLANES, ROWS, OWN_Y), shaped(8, OWN_Y * PLANES // 8), shaped(8, OWN_Y * PLANES // 8)),
        in_specs=[SMEM] + [VMEM] * 3,
        out_specs=(VMEM,) * 3,
        compiler_params=limit,
        name="strip",
    )(edge, own, low, high)
    from_left = ring(right, "gy", 1)
    from_right = ring(left, "gy", -1)

    def planes(*lead):
        return pltpu.VMEM(lead + (ROWS, LANES), jnp.float32)

    gram, mixes = pl.pallas_call(
        moments_kernel,
        out_shape=(shaped(16, 128), shaped(32, OWN_X, OWN_Y)),
        in_specs=[SMEM] + [VMEM] * 4,
        out_specs=(VMEM,) * 2,
        scratch_shapes=[
            planes(PLANES),
            pltpu.VMEM((24, OWN_Y), jnp.float32),
            planes(11),
            planes(11),
            planes(11),
            planes(11),
            planes(11),
            planes(12),
            planes(2, 11),
            planes(2, 11),
            planes(4, 11),
            pltpu.VMEM((4, 11, OWN_X, OWN_Y), jnp.float32),
            planes(4, 4, 11),
            pltpu.VMEM((4, 51, OWN_X, OWN_Y), jnp.float32),
            planes(2, 16),
            pltpu.VMEM((5, 128, OWN_Y), jnp.float32),
            pltpu.VMEM((5, 256, OWN_Y), jnp.float32),
        ],
        compiler_params=limit,
        name="moments",
    )(edge, tall, high, from_left, from_right)
    gram = spread_sum(spread_sum(gram, "gx"), "gy")
    return pl.pallas_call(
        finish_kernel,
        out_shape=shaped(8, OWN_X, OWN_Y),
        in_specs=[VMEM] * 2,
        out_specs=VMEM,
        compiler_params=limit,
        name="finish",
    )(gram, mixes)


def solution(mesh):
    in_specs = (
        P(None, None, "gx", "gy"),
        P("gx", "gy"),
        P("gx", "gy"),
        P("gx", "gy"),
        P("gx", "gy"),
        P("gx", "gy"),
        P(None, "gx", "gy"),
    )
    out_specs = P(None, "gx", "gy")
    return jax.shard_map(body, mesh=mesh, in_specs=in_specs, out_specs=out_specs, check_vma=False)
```

```python
import functools

import jax
import jax.numpy as jnp
from jax import lax
from jax.experimental import pallas as pl
from jax.experimental.pallas import tpu as pltpu
from jax.sharding import PartitionSpec as P

MASS_TERM = 0.1
STRAIN_OFFSET = 0.01
PRECISE = lax.Precision.HIGHEST

ROWS = 16
LANES = 256
OWN_X = 8
OWN_Y = 128
LOW = 4
THICK, MASK, FRIC, OBS, PROBE = 22, 23, 24, 25, 26
PLANES = 40


def dot(left, right, dims=((1,), (0,))):
    return lax.dot_general(
        left, right, (dims, ((), ())), precision=PRECISE, preferred_element_type=jnp.float32
    )


def shift(plane, step, axis):
    size = plane.shape[axis]
    return pltpu.roll(plane, (-step) % size, axis)


def pack_kernel(vel, thick, logf, obs, mask, ground, probes, own, up, down, land, land_int, sems):
    moves = [
        (vel.at[0], own.at[pl.ds(0, 11)]),
        (vel.at[1], own.at[pl.ds(11, 11)]),
        (thick, own.at[THICK]),
        (probes, own.at[pl.ds(PROBE, 8)]),
        (logf, land.at[0]),
        (obs, land.at[1]),
        (mask, land_int.at[0]),
        (ground, land_int.at[1]),
    ]
    copies = [pltpu.make_async_copy(src, dst, sems.at[k]) for k, (src, dst) in enumerate(moves)]
    for copy in copies:
        copy.start()
    for copy in copies:
        copy.wait()
    m = land_int[0].astype(jnp.float32)
    own[MASK] = m
    own[FRIC] = m * land_int[1].astype(jnp.float32) * jnp.exp(land[0])
    own[OBS] = land[1] * m
    for k in range(34):
        up[pl.ds(LOW * k, LOW), :] = own[k, OWN_X - LOW :, :]
        down[pl.ds(LOW * k, LOW), :] = own[k, :LOW, :]
        if k < 22:
            down[pl.ds(LOW * PLANES + k, 1), :] = own[k, LOW : LOW + 1, :]


def strip_kernel(edge, own, low, high, tall, left, right):
    keep_low = jnp.where(edge[0] == 0, 0.0, 1.0)
    keep_high = jnp.where(edge[1] == 0, 0.0, 1.0)
    for k in range(34):
        tall[k, 0:OWN_X, :] = own[k]
        tall[k, OWN_X : OWN_X + LOW, :] = high[pl.ds(LOW * k, LOW), :] * keep_high
        tall[k, ROWS - LOW : ROWS, :] = low[pl.ds(LOW * k, LOW), :] * keep_low
    for k in range(34, PLANES):
        tall[k] = jnp.zeros((ROWS, OWN_Y), jnp.float32)
    for b in range(PLANES // 8):
        turned = tall[8 * b : 8 * b + 8].reshape(8 * ROWS, OWN_Y).T
        left[:, OWN_Y * b : OWN_Y * (b + 1)] = turned[0:8]
        right[:, OWN_Y * b : OWN_Y * (b + 1)] = turned[OWN_Y - 8 : OWN_Y]


def moments_kernel(
    edge, tall, high, from_left, from_right, gram, mixes,
    full, row12, mu, kx, kxm, ky, kym, kz, inv, ratio, resp, phi, gam, wts, basis, lhs, rhs,
):
    keep_left = jnp.where(edge[2] == 0, 0.0, 1.0)
    keep_right = jnp.where(edge[3] == 0, 0.0, 1.0)
    keep_high = jnp.where(edge[1] == 0, 0.0, 1.0)
    gap = jnp.zeros((OWN_Y - 16, OWN_Y), jnp.float32)
    for b in range(PLANES // 8):
        cols = slice(OWN_Y * b, OWN_Y * (b + 1))
        block = jnp.concatenate(
            [from_right[:, cols] * keep_right, gap, from_left[:, cols] * keep_left], axis=0
        )
        full[8 * b : 8 * b + 8, :, OWN_Y:] = block.T.reshape(8, ROWS, OWN_Y)
        full[8 * b : 8 * b + 8, :, :OWN_Y] = tall[8 * b : 8 * b + 8]
    row12[...] = high[pl.ds(LOW * PLANES, 24), :] * keep_high

    m = full[MASK]
    icy = m > 0.5
    thick = jnp.where(icy, full[THICK], 1.0)
    steep = 10.0 / thick
    half_steep = 0.5 * steep
    steep2 = 0.5 * steep * steep
    mm_x = 0.5 * (m * shift(m, 1, 0))
    mm_y = 0.5 * (m * shift(m, 1, 1))
    fric = full[FRIC]
    base = MASS_TERM * m + (1.0 - m)
    last = lax.broadcasted_iota(jnp.int32, (ROWS, LANES), 0) == OWN_X + LOW - 1

    for l in range(11):
        grads = []
        for c in range(2):
            w = full[11 * c + l]
            beyond = jnp.concatenate(
                [row12[11 * c + l : 11 * c + l + 1, :], jnp.zeros((1, OWN_Y), jnp.float32)], axis=1
            )
            ahead = jnp.where(last, jnp.broadcast_to(beyond, (ROWS, LANES)), shift(w, 1, 0))
            gx = 0.5 * (ahead - shift(w, -1, 0))
            gy = 0.5 * (shift(w, 1, 1) - shift(w, -1, 1))
            gz = (full[11 * c + min(l + 1, 10)] - full[11 * c + max(l - 1, 0)]) * half_steep
            grads.append((gx, gy, gz))
        (ux, uy, uz), (vx, vy, vz) = grads
        cross = uy + vx
        e2 = ux * ux + vy * vy + ux * vy + 0.25 * (cross * cross + uz * uz + vz * vz) + STRAIN_OFFSET
        mu[l] = jnp.where(icy, 0.5 * jnp.exp(jnp.log(e2) * (-1.0 / 3.0)), 0.0)

    kz[0] = jnp.zeros((ROWS, LANES), jnp.float32)
    kz[11] = jnp.zeros((ROWS, LANES), jnp.float32)
    for l in range(11):
        here = mu[l]
        ex = (here + shift(here, 1, 0)) * mm_x
        ey = (here + shift(here, 1, 1)) * mm_y
        kx[l] = ex
        ky[l] = ey
        kxm[l] = shift(ex, -1, 0)
        kym[l] = shift(ey, -1, 1)
        if l < 10:
            kz[l + 1] = (here + mu[l + 1]) * steep2

    for c in range(2):
        a, b = (4.0, 1.0) if c == 0 else (1.0, 4.0)
        source = fric * full[11 * c]
        last_ratio = None
        carry = None
        for l in range(11):
            main = a * (kx[l] + kxm[l]) + b * (ky[l] + kym[l]) + base + kz[l] + kz[l + 1]
            if l == 0:
                main = main + fric
            else:
                main = main - kz[l] * last_ratio
            recip = 1.0 / main
            last_ratio = kz[l + 1] * recip
            inv[c, l] = recip
            ratio[c, l] = last_ratio
            carry = (source if l == 0 else kz[l] * carry) * recip
            resp[c, l] = carry
        top = inv[c, 10]
        resp[2 + c, 10] = top
        for l in range(9, -1, -1):
            step = ratio[c, l]
            carry = resp[c, l] + step * carry
            resp[c, l] = carry
            top = step * top
            resp[2 + c, l] = top

    def one_kind(kc, _):
        c = lax.rem(kc, 2)
        a = jnp.where(c == 0, 4.0, 1.0)
        b = 5.0 - a
        carry = [None] * 4
        n1x = jnp.zeros((OWN_X, OWN_Y), jnp.float32)
        n1y = n1x
        for l in range(11):
            e = resp[kc, l]
            parts = [
                a * (kx[l] * shift(e, 1, 0)),
                a * (kxm[l] * shift(e, -1, 0)),
                b * (ky[l] * shift(e, 1, 1)),
                b * (kym[l] * shift(e, -1, 1)),
            ]
            scale = inv[c, l]
            for s in range(4):
                phi[s, l] = parts[s][:OWN_X, :OWN_Y]
                total = parts[s] if l == 0 else parts[s] + kz[l] * carry[s]
                carry[s] = total * scale
                gam[kc, s, l] = carry[s]
            n1x = n1x + (e * parts[0])[:OWN_X, :OWN_Y]
            n1y = n1y + (e * parts[2])[:OWN_X, :OWN_Y]
        wts[kc, 1] = n1x
        wts[kc, 2] = n1y
        for l in range(9, -1, -1):
            step = ratio[c, l]
            for s in range(4):
                carry[s] = gam[kc, s, l] + step * carry[s]
                gam[kc, s, l] = carry[s]
        own = (slice(0, OWN_X), slice(0, OWN_Y))
        acc = [None] * 16
        for l in range(11):
            f = [phi[s, l] for s in range(4)]
            g = [gam[kc, s, l][own] for s in range(4)]
            for s in range(4):
                for t in range(s, 4):
                    term = f[s] * g[t]
                    acc[4 * s + t] = term if l == 0 else acc[4 * s + t] + term
        for s in range(4):
            for t in range(4):
                wts[kc, 3 + 4 * s + t] = acc[4 * min(s, t) + max(s, t)]
        for way in range(2):
            acc = [None] * 16
            for l in range(11):
                edge_k = kx[l][own] * a if way == 0 else ky[l][own] * b
                g = [gam[kc, s, l][own] * edge_k for s in range(4)]
                if way == 0:
                    h = [shift(gam[kc, s, l, :, :OWN_Y], 1, 0)[:OWN_X] for s in range(4)]
                else:
                    h = [shift(gam[kc, s, l, :OWN_X, :], 1, 1)[:, :OWN_Y] for s in range(4)]
                for s in range(4):
                    for t in range(4):
                        term = g[s] * h[t]
                        acc[4 * s + t] = term if l == 0 else acc[4 * s + t] + term
            for s in range(16):
                wts[kc, 19 + 16 * way + s] = acc[s]
        return 0

    lax.fori_loop(0, 4, one_kind, 0)
    own = (slice(0, OWN_X), slice(0, OWN_Y))
    for c in range(2):
        source = (fric * full[11 * c])[own]
        wts[c, 0] = source * resp[c, 0][own]
        wts[2 + c, 0] = resp[2 + c, 10][own]
    for k in range(51):
        wts[0, k] = wts[0, k] + wts[1, k]

    obs = full[OBS]

    def one_probe(a, _):
        p = full[PROBE + a]
        near = [shift(p, 1, 0), shift(p, -1, 0), shift(p, 1, 1), shift(p, -1, 1)]
        for c in range(2):
            basis[c, a] = obs * resp[c, 10] * p
            total = gam[c, 0, 10] * near[0]
            for s in range(1, 4):
                total = total + gam[c, s, 10] * near[s]
            basis[c, 8 + a] = obs * total
        return 0

    lax.fori_loop(0, 8, one_probe, 0)

    def terms(kc, b, plane):
        mid = plane[:, :OWN_Y]
        yp = shift(plane, 1, 1)
        ym = shift(plane, -1, 1)[:, :OWN_Y]
        y2 = shift(yp[:OWN_X], 1, 1)[:, :OWN_Y]
        yp = yp[:, :OWN_Y]
        p00 = mid[:OWN_X]
        pxp, pxm, px2 = (shift(mid, d, 0)[:OWN_X] for d in (1, -1, 2))
        pyp, pxpyp, pxmyp = yp[:OWN_X], shift(yp, 1, 0)[:OWN_X], shift(yp, -1, 0)[:OWN_X]
        pym, pxpym = ym[:OWN_X], shift(ym, 1, 0)[:OWN_X]
        near = [pxp, pxm, pyp, pym]
        past_x = [px2, p00, pxpyp, pxpym]
        past_y = [pxpyp, pxmyp, y2, p00]
        return p00, near, past_x, past_y

    def fill(kc, b, plane, many):
        p00, near, past_x, past_y = terms(kc, b, plane)
        here = pl.ds(pl.multiple_of(OWN_X * b, OWN_X), OWN_X)
        there = pl.ds(pl.multiple_of(OWN_X * (many + b), OWN_X), OWN_X)
        for t in range(4):
            second = wts[kc, 3 + 4 * t] * near[0]
            for s in range(1, 4):
                second = second + wts[kc, 3 + 4 * t + s] * near[s]
            third = wts[kc, 19 + 4 * t] * past_x[0] + wts[kc, 35 + 4 * t] * past_y[0]
            for s in range(1, 4):
                third = third + wts[kc, 19 + 4 * t + s] * past_x[s]
                third = third + wts[kc, 35 + 4 * t + s] * past_y[s]
            lhs[t, here, :] = near[t]
            rhs[t, here, :] = second
            rhs[t, there, :] = third
        lhs[4, here, :] = p00
        rhs[4, here, :] = wts[kc, 0] * p00
        rhs[4, there, :] = wts[kc, 1] * near[0] + wts[kc, 2] * near[2]
        return p00, near

    def products(many):
        rows = OWN_X * many
        nt = ((1,), (1,))
        ends = dot(lhs[4, :rows, :], rhs[4, : 2 * rows, :], nt)
        sides = dot(lhs[0, :rows, :], rhs[0, : 2 * rows, :], nt)
        for t in range(1, 4):
            sides = sides + dot(lhs[t, :rows, :], rhs[t, : 2 * rows, :], nt)
        return ends, sides

    def fold(product, many):
        rows = OWN_X * many
        same = lax.broadcasted_iota(jnp.int32, (rows, 2 * rows), 0) % OWN_X == (
            lax.broadcasted_iota(jnp.int32, (rows, 2 * rows), 1) % OWN_X
        )
        kept = jnp.where(same, product, 0.0).reshape(many, OWN_X, 2 * rows)
        narrow = jnp.sum(kept, axis=1)
        pick = lax.broadcasted_iota(jnp.int32, (2 * rows, 2 * many), 0) // OWN_X == (
            lax.broadcasted_iota(jnp.int32, (2 * rows, 2 * many), 1)
        )
        return dot(narrow, jnp.where(pick, 1.0, 0.0))

    def fill_probe(b, _):
        fill(0, b, full[PROBE + b], 8)
        return 0

    lax.fori_loop(0, 8, fill_probe, 0)
    ends, sides = products(8)
    gram[:, 96:128] = jnp.zeros((8, 32), jnp.float32)
    gram[:, 96:114] = joined(fold(ends, 8), fold(sides, 8))

    total_ends = total_sides = None
    for c in range(2):
        weight = (fric * full[11 * c])[own]

        def fill_basis(b, _, c=c, weight=weight):
            p00, near = fill(2 + c, b, basis[c, b], 16)
            one = weight * resp[2 + c, 0, :OWN_X, :OWN_Y] * p00
            two = gam[2 + c, 0, 0, :OWN_X, :OWN_Y] * near[0]
            for s in range(1, 4):
                two = two + gam[2 + c, s, 0, :OWN_X, :OWN_Y] * near[s]
            two = weight * two
            if c == 1:
                one = one + mixes[b]
                two = two + mixes[16 + b]
            mixes[b] = one
            mixes[16 + b] = two
            return 0

        lax.fori_loop(0, 16, fill_basis, 0)
        ends, sides = products(16)
        total_ends = ends if c == 0 else total_ends + ends
        total_sides = sides if c == 0 else total_sides + sides
    pair = joined(fold(total_ends, 16), fold(total_sides, 16))
    gram[:, 0:34] = pair[0:8]
    gram[:, 34:48] = jnp.zeros((8, 14), jnp.float32)
    gram[:, 48:82] = pair[8:16]
    gram[:, 82:96] = jnp.zeros((8, 14), jnp.float32)


def places(rows, cols):
    return lax.broadcasted_iota(jnp.int32, (rows, cols), 0), lax.broadcasted_iota(jnp.int32, (rows, cols), 1)


def turned(square):
    row, col = places(square.shape[0], square.shape[0])
    return dot(jnp.where(row == col, 1.0, 0.0), square, ((1,), (1,)))


def joined(ends, sides):
    size = ends.shape[0]
    row, col = places(size, size)
    squares, lines = [], []
    for both in (ends, sides):
        half = both[:, size:]
        whole = half + turned(half)
        squares.append(jnp.where(row <= col, both[:, :size], whole))
        lines.append(jnp.sum(jnp.where(row == col, whole, 0.0), axis=1, keepdims=True))
    return jnp.concatenate(squares + lines, axis=1)


def parted(packed):
    size = packed.shape[0]
    row, col = places(size, size)
    found = []
    for k in range(2):
        square = packed[:, size * k : size * (k + 1)]
        other = turned(square)
        line = packed[:, 2 * size + k : 2 * size + k + 1]
        found.append(jnp.where(row <= col, square, other))
        found.append(jnp.where(row > col, square, jnp.where(row == col, line, other)))
    return found


def krylov_solve(moments, sides):
    m0, m1, m2, m3 = moments
    low = m1 - m2
    square = jnp.concatenate(
        [jnp.concatenate([m0 - m1, low], axis=1), jnp.concatenate([low, m2 - m3], axis=1)], axis=0
    )
    row, col = places(16, 16)
    kept = jnp.where(row == col, square, 0.0)
    tall, wide = jnp.sum(kept, axis=1, keepdims=True), jnp.sum(kept, axis=0, keepdims=True)
    tall = jnp.where(tall > 0.0, lax.rsqrt(tall), 0.0)
    wide = jnp.where(wide > 0.0, lax.rsqrt(wide), 0.0)
    square = jnp.where((row == col) & (tall == 0.0), 1.0, square * tall * wide)
    system = jnp.concatenate([square, jnp.concatenate(sides, axis=0) * tall], axis=1)
    row, _ = places(*system.shape)
    for k in range(0, 16, 2):
        one, two = system[k : k + 1, :], system[k + 1 : k + 2, :]
        left = jnp.broadcast_to(system[:, k : k + 1], system.shape)
        right = jnp.broadcast_to(system[:, k + 1 : k + 2], system.shape)
        p, q = left[k : k + 1, :], right[k : k + 1, :]
        r, t = left[k + 1 : k + 2, :], right[k + 1 : k + 2, :]
        scale = 1.0 / (p * t - q * r)
        first = (t * one - q * two) * scale
        second = (p * two - r * one) * scale
        rest = system - left * first - right * second
        system = jnp.where(row == k, first, jnp.where(row == k + 1, second, rest))
    return system[:, 16:] * tall


def raised(coef):
    rows, cols = coef.shape
    tall = jnp.broadcast_to(coef[:, None, :], (rows, OWN_X, cols)).reshape(rows * OWN_X, cols)
    row, col = places(rows * OWN_X, cols)
    return jnp.where(row % OWN_X == col % OWN_X, tall, 0.0)


def finish_kernel(gram, mixes, out):
    tn = ((0,), (0,))
    row, col = places(8, 64)
    repeat = jnp.where(col // 8 == row, 1.0, 0.0)
    first = parted(gram[:, 96:114])
    wide = krylov_solve(first, [dot(first[0], repeat), dot(first[1], repeat)])
    row, col = places(64, 8)
    mix = dot(wide, jnp.where(row == 8 * col, 1.0, 0.0))
    adjoint = parted(jnp.concatenate([gram[:, 0:34], gram[:, 48:82]], axis=0))
    half = dot(mix, jnp.concatenate(adjoint, axis=1), tn)
    halves = [half[:, 16 * k : 16 * k + 16] for k in range(4)]
    second = [dot(part, mix) for part in halves]
    coef = krylov_solve(second, [dot(halves[0], wide), dot(halves[1], wide)])
    spread = raised(wide)
    flat = jnp.concatenate([dot(spread, mixes[16 * k : 16 * k + 16].reshape(128, OWN_Y), tn) for k in range(2)], axis=0)
    out[...] = dot(raised(coef), flat, tn).reshape(8, OWN_X, OWN_Y)


VMEM = pl.BlockSpec(memory_space=pltpu.VMEM)
SMEM = pl.BlockSpec(memory_space=pltpu.SMEM)


def shaped(*dims):
    return jax.ShapeDtypeStruct(dims, jnp.float32)


def spread_sum(values, axis):
    count = lax.axis_size(axis)
    copies = jnp.broadcast_to(values, (count,) + values.shape)
    return jnp.sum(lax.all_to_all(copies, axis, 0, 0), axis=0)


def ring(values, axis, step):
    count = lax.axis_size(axis)
    return lax.ppermute(values, axis, [(i, (i + step) % count) for i in range(count)])


def body(velocity, thickness, log_friction, obs_weight, ice_mask, grounded, probes):
    at_x, at_y = lax.axis_index("gx"), lax.axis_index("gy")
    edge = jnp.stack(
        [at_x, lax.axis_size("gx") - 1 - at_x, at_y, lax.axis_size("gy") - 1 - at_y]
    ).astype(jnp.int32)
    limit = pltpu.CompilerParams(vmem_limit_bytes=48 * 1024 * 1024)
    own, up, down = pl.pallas_call(
        pack_kernel,
        out_shape=(shaped(PLANES, OWN_X, OWN_Y), shaped(LOW * PLANES, OWN_Y), shaped(LOW * PLANES + 24, OWN_Y)),
        in_specs=[pl.BlockSpec(memory_space=pl.ANY)] * 7,
        out_specs=(VMEM,) * 3,
        scratch_shapes=[
            pltpu.VMEM((2, OWN_X, OWN_Y), jnp.float32),
            pltpu.VMEM((2, OWN_X, OWN_Y), jnp.int32),
            pltpu.SemaphoreType.DMA((8,)),
        ],
        compiler_params=limit,
        name="pack",
    )(velocity, thickness, log_friction, obs_weight, ice_mask, grounded, probes)
    low = ring(up, "gx", 1)
    high = ring(down, "gx", -1)
    tall, left, right = pl.pallas_call(
        strip_kernel,
        out_shape=(shaped(PLANES, ROWS, OWN_Y), shaped(8, OWN_Y * PLANES // 8), shaped(8, OWN_Y * PLANES // 8)),
        in_specs=[SMEM] + [VMEM] * 3,
        out_specs=(VMEM,) * 3,
        compiler_params=limit,
        name="strip",
    )(edge, own, low, high)
    from_left = ring(right, "gy", 1)
    from_right = ring(left, "gy", -1)

    def planes(*lead):
        return pltpu.VMEM(lead + (ROWS, LANES), jnp.float32)

    gram, mixes = pl.pallas_call(
        moments_kernel,
        out_shape=(shaped(8, 128), shaped(32, OWN_X, OWN_Y)),
        in_specs=[SMEM] + [VMEM] * 4,
        out_specs=(VMEM,) * 2,
        scratch_shapes=[
            planes(PLANES),
            pltpu.VMEM((24, OWN_Y), jnp.float32),
            planes(11),
            planes(11),
            planes(11),
            planes(11),
            planes(11),
            planes(12),
            planes(2, 11),
            planes(2, 11),
            planes(4, 11),
            pltpu.VMEM((4, 11, OWN_X, OWN_Y), jnp.float32),
            planes(4, 4, 11),
            pltpu.VMEM((4, 51, OWN_X, OWN_Y), jnp.float32),
            planes(2, 16),
            pltpu.VMEM((5, 128, OWN_Y), jnp.float32),
            pltpu.VMEM((5, 256, OWN_Y), jnp.float32),
        ],
        compiler_params=limit,
        name="moments",
    )(edge, tall, high, from_left, from_right)
    gram = spread_sum(spread_sum(gram, "gx"), "gy")
    return pl.pallas_call(
        finish_kernel,
        out_shape=shaped(8, OWN_X, OWN_Y),
        in_specs=[VMEM] * 2,
        out_specs=VMEM,
        compiler_params=limit,
        name="finish",
    )(gram, mixes)


def solution(mesh):
    in_specs = (
        P(None, None, "gx", "gy"),
        P("gx", "gy"),
        P("gx", "gy"),
        P("gx", "gy"),
        P("gx", "gy"),
        P("gx", "gy"),
        P(None, "gx", "gy"),
    )
    out_specs = P(None, "gx", "gy")
    return jax.shard_map(body, mesh=mesh, in_specs=in_specs, out_specs=out_specs, check_vma=False)
```

```python
import functools

import jax
import jax.numpy as jnp
from jax import lax
from jax.experimental import pallas as pl
from jax.experimental.pallas import tpu as pltpu
from jax.sharding import PartitionSpec as P

MASS_TERM = 0.1
STRAIN_OFFSET = 0.01
PRECISE = lax.Precision.HIGHEST

ROWS = 16
LANES = 256
OWN_X = 8
OWN_Y = 128
LOW = 4
THICK, MASK, FRIC, OBS, PROBE = 22, 23, 24, 25, 26
PLANES = 40


def dot(left, right, dims=((1,), (0,))):
    return lax.dot_general(
        left, right, (dims, ((), ())), precision=PRECISE, preferred_element_type=jnp.float32
    )


def shift(plane, step, axis):
    size = plane.shape[axis]
    return pltpu.roll(plane, (-step) % size, axis)


def pack_kernel(own, up, down):
    for k in range(34):
        up[pl.ds(LOW * k, LOW), :] = own[k, OWN_X - LOW :, :]
        down[pl.ds(LOW * k, LOW), :] = own[k, :LOW, :]
        if k < 22:
            down[pl.ds(LOW * PLANES + k, 1), :] = own[k, LOW : LOW + 1, :]


def strip_kernel(edge, own, low, high, tall, left, right):
    keep_low = jnp.where(edge[0] == 0, 0.0, 1.0)
    keep_high = jnp.where(edge[1] == 0, 0.0, 1.0)
    for k in range(34):
        tall[k, 0:OWN_X, :] = own[k]
        tall[k, OWN_X : OWN_X + LOW, :] = high[pl.ds(LOW * k, LOW), :] * keep_high
        tall[k, ROWS - LOW : ROWS, :] = low[pl.ds(LOW * k, LOW), :] * keep_low
    for k in range(34, PLANES):
        tall[k] = jnp.zeros((ROWS, OWN_Y), jnp.float32)
    for b in range(PLANES // 8):
        turned = tall[8 * b : 8 * b + 8].reshape(8 * ROWS, OWN_Y).T
        left[:, OWN_Y * b : OWN_Y * (b + 1)] = turned[0:8]
        right[:, OWN_Y * b : OWN_Y * (b + 1)] = turned[OWN_Y - 8 : OWN_Y]


def moments_kernel(
    edge, tall, high, from_left, from_right, gram, mixes,
    full, row12, mu, kx, kxm, ky, kym, kz, inv, ratio, resp, phi, gam, wts, basis,
    lhs8, rhs8, lhs16, rhs16,
):
    keep_left = jnp.where(edge[2] == 0, 0.0, 1.0)
    keep_right = jnp.where(edge[3] == 0, 0.0, 1.0)
    keep_high = jnp.where(edge[1] == 0, 0.0, 1.0)
    gap = jnp.zeros((OWN_Y - 16, OWN_Y), jnp.float32)
    for b in range(PLANES // 8):
        cols = slice(OWN_Y * b, OWN_Y * (b + 1))
        block = jnp.concatenate(
            [from_right[:, cols] * keep_right, gap, from_left[:, cols] * keep_left], axis=0
        )
        full[8 * b : 8 * b + 8, :, OWN_Y:] = block.T.reshape(8, ROWS, OWN_Y)
        full[8 * b : 8 * b + 8, :, :OWN_Y] = tall[8 * b : 8 * b + 8]
    row12[...] = high[pl.ds(LOW * PLANES, 24), :] * keep_high

    m = full[MASK]
    icy = m > 0.5
    thick = jnp.where(icy, full[THICK], 1.0)
    steep = 10.0 / thick
    half_steep = 0.5 * steep
    steep2 = 0.5 * steep * steep
    mm_x = 0.5 * (m * shift(m, 1, 0))
    mm_y = 0.5 * (m * shift(m, 1, 1))
    fric = full[FRIC]
    base = MASS_TERM * m + (1.0 - m)
    last = lax.broadcasted_iota(jnp.int32, (ROWS, LANES), 0) == OWN_X + LOW - 1

    for l in range(11):
        grads = []
        for c in range(2):
            w = full[11 * c + l]
            beyond = jnp.concatenate(
                [row12[11 * c + l : 11 * c + l + 1, :], jnp.zeros((1, OWN_Y), jnp.float32)], axis=1
            )
            ahead = jnp.where(last, jnp.broadcast_to(beyond, (ROWS, LANES)), shift(w, 1, 0))
            gx = 0.5 * (ahead - shift(w, -1, 0))
            gy = 0.5 * (shift(w, 1, 1) - shift(w, -1, 1))
            gz = (full[11 * c + min(l + 1, 10)] - full[11 * c + max(l - 1, 0)]) * half_steep
            grads.append((gx, gy, gz))
        (ux, uy, uz), (vx, vy, vz) = grads
        cross = uy + vx
        e2 = ux * ux + vy * vy + ux * vy + 0.25 * (cross * cross + uz * uz + vz * vz) + STRAIN_OFFSET
        mu[l] = jnp.where(icy, 0.5 * jnp.exp(jnp.log(e2) * (-1.0 / 3.0)), 0.0)

    kz[0] = jnp.zeros((ROWS, LANES), jnp.float32)
    kz[11] = jnp.zeros((ROWS, LANES), jnp.float32)
    for l in range(11):
        here = mu[l]
        ex = (here + shift(here, 1, 0)) * mm_x
        ey = (here + shift(here, 1, 1)) * mm_y
        kx[l] = ex
        ky[l] = ey
        kxm[l] = shift(ex, -1, 0)
        kym[l] = shift(ey, -1, 1)
        if l < 10:
            kz[l + 1] = (here + mu[l + 1]) * steep2

    for c in range(2):
        a, b = (4.0, 1.0) if c == 0 else (1.0, 4.0)
        source = fric * full[11 * c]
        last_ratio = None
        carry = None
        for l in range(11):
            main = a * (kx[l] + kxm[l]) + b * (ky[l] + kym[l]) + base + kz[l] + kz[l + 1]
            if l == 0:
                main = main + fric
            else:
                main = main - kz[l] * last_ratio
            recip = 1.0 / main
            last_ratio = kz[l + 1] * recip
            inv[c, l] = recip
            ratio[c, l] = last_ratio
            carry = (source if l == 0 else kz[l] * carry) * recip
            resp[c, l] = carry
        top = inv[c, 10]
        resp[2 + c, 10] = top
        for l in range(9, -1, -1):
            step = ratio[c, l]
            carry = resp[c, l] + step * carry
            resp[c, l] = carry
            top = step * top
            resp[2 + c, l] = top

    def one_kind(kc, _):
        c = lax.rem(kc, 2)
        a = jnp.where(c == 0, 4.0, 1.0)
        b = 5.0 - a
        carry = [None] * 4
        n1 = [None] * 4
        for l in range(11):
            e = resp[kc, l]
            parts = [
                a * (kx[l] * shift(e, 1, 0)),
                a * (kxm[l] * shift(e, -1, 0)),
                b * (ky[l] * shift(e, 1, 1)),
                b * (kym[l] * shift(e, -1, 1)),
            ]
            scale = inv[c, l]
            for s in range(4):
                phi[s, l] = parts[s][:OWN_X, :OWN_Y]
                total = parts[s] if l == 0 else parts[s] + kz[l] * carry[s]
                carry[s] = total * scale
                gam[kc, s, l] = carry[s]
            for s in range(4):
                term = (e * parts[s])[:OWN_X, :OWN_Y]
                n1[s] = term if l == 0 else n1[s] + term
        for s in range(4):
            wts[kc, 1 + s] = n1[s]
        for l in range(9, -1, -1):
            step = ratio[c, l]
            for s in range(4):
                carry[s] = gam[kc, s, l] + step * carry[s]
                gam[kc, s, l] = carry[s]
        own = (slice(0, OWN_X), slice(0, OWN_Y))
        acc = [None] * 16
        for l in range(11):
            f = [phi[s, l] for s in range(4)]
            g = [gam[kc, s, l][own] for s in range(4)]
            for s in range(4):
                for t in range(s, 4):
                    term = f[s] * g[t]
                    acc[4 * s + t] = term if l == 0 else acc[4 * s + t] + term
        for s in range(4):
            for t in range(4):
                wts[kc, 5 + 4 * s + t] = acc[4 * min(s, t) + max(s, t)]
        for way in range(2):
            acc = [None] * 16
            for l in range(11):
                edge_k = kx[l][own] * a if way == 0 else ky[l][own] * b
                g = [gam[kc, s, l][own] * edge_k for s in range(4)]
                if way == 0:
                    h = [shift(gam[kc, s, l, :, :OWN_Y], 1, 0)[:OWN_X] for s in range(4)]
                else:
                    h = [shift(gam[kc, s, l, :OWN_X, :], 1, 1)[:, :OWN_Y] for s in range(4)]
                for s in range(4):
                    for t in range(4):
                        term = g[s] * h[t]
                        acc[4 * s + t] = term if l == 0 else acc[4 * s + t] + term
            for s in range(16):
                wts[kc, 21 + 16 * way + s] = acc[s]
        return 0

    lax.fori_loop(0, 4, one_kind, 0)
    own = (slice(0, OWN_X), slice(0, OWN_Y))
    for c in range(2):
        source = (fric * full[11 * c])[own]
        wts[c, 0] = source * resp[c, 0][own]
        wts[2 + c, 0] = resp[2 + c, 10][own]
    for k in range(53):
        wts[0, k] = wts[0, k] + wts[1, k]

    obs = full[OBS]

    def one_probe(a, _):
        p = full[PROBE + a]
        near = [shift(p, 1, 0), shift(p, -1, 0), shift(p, 1, 1), shift(p, -1, 1)]
        for c in range(2):
            basis[c, a] = obs * resp[c, 10] * p
            total = gam[c, 0, 10] * near[0]
            for s in range(1, 4):
                total = total + gam[c, s, 10] * near[s]
            basis[c, 8 + a] = obs * total
        return 0

    lax.fori_loop(0, 8, one_probe, 0)

    def shifted(plane):
        mid = plane[:, :OWN_Y]
        yp = shift(plane, 1, 1)
        ym = shift(plane, -1, 1)[:, :OWN_Y]
        y2 = shift(yp[:OWN_X], 1, 1)[:, :OWN_Y]
        yp = yp[:, :OWN_Y]
        p00 = mid[:OWN_X]
        pxp, pxm, px2 = (shift(mid, d, 0)[:OWN_X] for d in (1, -1, 2))
        pyp, pxpyp, pxmyp = yp[:OWN_X], shift(yp, 1, 0)[:OWN_X], shift(yp, -1, 0)[:OWN_X]
        pym, pxpym = ym[:OWN_X], shift(ym, 1, 0)[:OWN_X]
        return p00, [pxp, pxm, pyp, pym], [px2, p00, pxpyp, pxpym], [pxpyp, pxmyp, y2, p00]

    def fill(kc, b, plane, many, lhs, rhs, first):
        p00, near, past_x, past_y = shifted(plane)
        here = pl.ds(b, OWN_X, stride=many)
        one = pl.ds(b, OWN_X, stride=2 * many)
        two = pl.ds(many + b, OWN_X, stride=2 * many)
        for t in range(4):
            second = wts[kc, 5 + 4 * t] * near[0]
            for s in range(1, 4):
                second = second + wts[kc, 5 + 4 * t + s] * near[s]
            third = wts[kc, 21 + 4 * t] * past_x[0] + wts[kc, 37 + 4 * t] * past_y[0]
            for s in range(1, 4):
                third = third + wts[kc, 21 + 4 * t + s] * past_x[s]
                third = third + wts[kc, 37 + 4 * t + s] * past_y[s]
            lhs[first + t, here, :] = near[t]
            rhs[first + t, one, :] = second
            rhs[first + t, two, :] = third
        lhs[first + 4, here, :] = p00
        rhs[first + 4, one, :] = wts[kc, 0] * p00
        side = wts[kc, 1] * near[0]
        for s in range(1, 4):
            side = side + wts[kc, 1 + s] * near[s]
        rhs[first + 4, two, :] = side
        return p00, near

    def side_by_side(ref, which):
        return jnp.concatenate([ref[k] for k in which], axis=1)

    def fold(lhs, rhs, which, many):
        product = dot(side_by_side(lhs, which), side_by_side(rhs, which), ((1,), (1,)))
        row, col = places(OWN_X * many, 2 * OWN_X * many)
        product = jnp.where(row // many == col // (2 * many), product, 0.0)
        total = jnp.sum(product.reshape(OWN_X, many, 2 * OWN_X * many), axis=0)
        if many == 16:
            total = total[:, :128] + total[:, 128:]
        step = 64
        while step >= 2 * many:
            total = total + pltpu.roll(total, step, 1)
            step //= 2
        return total

    def fill_probe(pair, _):
        for b in (2 * pair, 2 * pair + 1):
            fill(0, b, full[PROBE + b], 8, lhs8, rhs8, 0)
        return 0

    lax.fori_loop(0, 4, fill_probe, 0)

    weights = [(fric * full[11 * c])[own] for c in range(2)]

    def fill_basis(b, _):
        one = two = None
        for c in range(2):
            p00, near = fill(2 + c, b, basis[c, b], 16, lhs16, rhs16, 5 * c)
            here = resp[2 + c, 0, :OWN_X, :OWN_Y] * p00
            there = gam[2 + c, 0, 0, :OWN_X, :OWN_Y] * near[0]
            for s in range(1, 4):
                there = there + gam[2 + c, s, 0, :OWN_X, :OWN_Y] * near[s]
            one = weights[c] * here if c == 0 else one + weights[c] * here
            two = weights[c] * there if c == 0 else two + weights[c] * there
        mixes[b] = one
        mixes[16 + b] = two
        return 0

    lax.fori_loop(0, 16, fill_basis, 0)

    ends8, sides8 = fold(lhs8, rhs8, (4,), 8), fold(lhs8, rhs8, (0, 1, 2, 3), 8)
    ends16, sides16 = fold(lhs16, rhs16, (4, 9), 16), fold(lhs16, rhs16, (0, 1, 2, 3, 5, 6, 7, 8), 16)

    def woven(ends, many):
        row, col = places(many, 128)
        other = pltpu.roll(ends, 128 - many, 1)
        line = jnp.sum(jnp.where(row == col, other, 0.0), axis=1, keepdims=True)
        return jnp.where(row <= col, ends, other), line

    square16, line16 = woven(ends16, 16)
    square8, line8 = woven(ends8, 8)
    _, col = places(16, 128)
    tall16 = jnp.where(col < 16, square16, pltpu.roll(sides16, 16, 1))
    _, col = places(8, 128)
    message = jnp.where(col < 48, tall16[:8], pltpu.roll(tall16[8:], 48, 1))
    message = jnp.where(col < 96, message, pltpu.roll(square8, 96, 1))
    message = jnp.where(col < 104, message, pltpu.roll(sides8, 104, 1))
    message = jnp.where(col < 120, message, line16[:8])
    message = jnp.where(col < 121, message, line16[8:])
    message = jnp.where(col < 122, message, line8)
    gram[...] = jnp.where(col < 123, message, 0.0)


def places(rows, cols):
    return lax.broadcasted_iota(jnp.int32, (rows, cols), 0), lax.broadcasted_iota(jnp.int32, (rows, cols), 1)


def turned(square):
    row, col = places(square.shape[0], square.shape[0])
    return dot(jnp.where(row == col, 1.0, 0.0), square, ((1,), (1,)))


def parted(packed, line):
    size = packed.shape[0]
    row, col = places(size, size)
    square = packed[:, :size]
    other = turned(square)
    half = packed[:, 2 * size : 3 * size]
    return (
        jnp.where(row <= col, square, other),
        jnp.where(row > col, square, jnp.where(row == col, line, other)),
        packed[:, size : 2 * size],
        half + turned(half),
    )


def krylov_solve(moments, sides):
    m0, m1, m2, m3 = moments
    low = m1 - m2
    square = jnp.concatenate(
        [jnp.concatenate([m0 - m1, low], axis=1), jnp.concatenate([low, m2 - m3], axis=1)], axis=0
    )
    row, col = places(16, 16)
    kept = jnp.where(row == col, square, 0.0)
    tall, wide = jnp.sum(kept, axis=1, keepdims=True), jnp.sum(kept, axis=0, keepdims=True)
    tall = jnp.where(tall > 0.0, lax.rsqrt(tall), 0.0)
    wide = jnp.where(wide > 0.0, lax.rsqrt(wide), 0.0)
    square = jnp.where((row == col) & (tall == 0.0), 1.0, square * tall * wide)
    system = jnp.concatenate([square, jnp.concatenate(sides, axis=0) * tall], axis=1)
    row, _ = places(*system.shape)
    for k in range(0, 16, 2):
        one, two = system[k : k + 1, :], system[k + 1 : k + 2, :]
        left = jnp.broadcast_to(system[:, k : k + 1], system.shape)
        right = jnp.broadcast_to(system[:, k + 1 : k + 2], system.shape)
        p, q = left[k : k + 1, :], right[k : k + 1, :]
        r, t = left[k + 1 : k + 2, :], right[k + 1 : k + 2, :]
        scale = 1.0 / (p * t - q * r)
        first = (t * one - q * two) * scale
        second = (p * two - r * one) * scale
        rest = system - left * first - right * second
        system = jnp.where(row == k, first, jnp.where(row == k + 1, second, rest))
    return system[:, 16:] * tall


def raised(coef):
    rows, cols = coef.shape
    tall = jnp.broadcast_to(coef[:, None, :], (rows, OWN_X, cols)).reshape(rows * OWN_X, cols)
    row, col = places(rows * OWN_X, cols)
    return jnp.where(row % OWN_X == col % OWN_X, tall, 0.0)


def finish_kernel(gram, mixes, out):
    tn = ((0,), (0,))
    row, col = places(8, 64)
    repeat = jnp.where(col // 8 == row, 1.0, 0.0)
    first = parted(gram[:, 96:120], gram[:, 122:123])
    wide = krylov_solve(first, [dot(first[0], repeat), dot(first[1], repeat)])
    row, col = places(64, 8)
    mix = dot(wide, jnp.where(row == 8 * col, 1.0, 0.0))
    adjoint = parted(
        jnp.concatenate([gram[:, 0:48], gram[:, 48:96]], axis=0),
        jnp.concatenate([gram[:, 120:121], gram[:, 121:122]], axis=0),
    )
    half = dot(mix, jnp.concatenate(adjoint, axis=1), tn)
    halves = [half[:, 16 * k : 16 * k + 16] for k in range(4)]
    second = [dot(part, mix) for part in halves]
    coef = krylov_solve(second, [dot(halves[0], wide), dot(halves[1], wide)])
    spread = raised(wide)
    flat = jnp.concatenate([dot(spread, mixes[16 * k : 16 * k + 16].reshape(128, OWN_Y), tn) for k in range(2)], axis=0)
    out[...] = dot(raised(coef), flat, tn).reshape(8, OWN_X, OWN_Y)


VMEM = pl.BlockSpec(memory_space=pltpu.VMEM)
SMEM = pl.BlockSpec(memory_space=pltpu.SMEM)


def shaped(*dims):
    return jax.ShapeDtypeStruct(dims, jnp.float32)


def spread_sum(values, axis):
    count = lax.axis_size(axis)
    copies = jnp.broadcast_to(values, (count,) + values.shape)
    return jnp.sum(lax.all_to_all(copies, axis, 0, 0), axis=0)


def ring(values, axis, step):
    count = lax.axis_size(axis)
    return lax.ppermute(values, axis, [(i, (i + step) % count) for i in range(count)])


def body(velocity, thickness, log_friction, obs_weight, ice_mask, grounded, probes):
    at_x, at_y = lax.axis_index("gx"), lax.axis_index("gy")
    edge = jnp.stack(
        [at_x, lax.axis_size("gx") - 1 - at_x, at_y, lax.axis_size("gy") - 1 - at_y]
    ).astype(jnp.int32)
    limit = pltpu.CompilerParams(vmem_limit_bytes=48 * 1024 * 1024)
    mask = ice_mask.astype(jnp.float32)
    friction = mask * grounded.astype(jnp.float32) * jnp.exp(log_friction)
    fields = jnp.stack([thickness, mask, friction, obs_weight * mask])
    own = jnp.concatenate([velocity.reshape(22, OWN_X, OWN_Y), fields, probes], axis=0)
    up, down = pl.pallas_call(
        pack_kernel,
        out_shape=(shaped(LOW * PLANES, OWN_Y), shaped(LOW * PLANES + 24, OWN_Y)),
        in_specs=[VMEM],
        out_specs=(VMEM,) * 2,
        compiler_params=limit,
        name="pack",
    )(own)
    low = ring(up, "gx", 1)
    high = ring(down, "gx", -1)
    tall, left, right = pl.pallas_call(
        strip_kernel,
        out_shape=(shaped(PLANES, ROWS, OWN_Y), shaped(8, OWN_Y * PLANES // 8), shaped(8, OWN_Y * PLANES // 8)),
        in_specs=[SMEM] + [VMEM] * 3,
        out_specs=(VMEM,) * 3,
        compiler_params=limit,
        name="strip",
    )(edge, own, low, high)
    from_left = ring(right, "gy", 1)
    from_right = ring(left, "gy", -1)

    def planes(*lead):
        return pltpu.VMEM(lead + (ROWS, LANES), jnp.float32)

    gram, mixes = pl.pallas_call(
        moments_kernel,
        out_shape=(shaped(8, 128), shaped(32, OWN_X, OWN_Y)),
        in_specs=[SMEM] + [VMEM] * 4,
        out_specs=(VMEM,) * 2,
        scratch_shapes=[
            planes(PLANES),
            pltpu.VMEM((24, OWN_Y), jnp.float32),
            planes(11),
            planes(11),
            planes(11),
            planes(11),
            planes(11),
            planes(12),
            planes(2, 11),
            planes(2, 11),
            planes(4, 11),
            pltpu.VMEM((4, 11, OWN_X, OWN_Y), jnp.float32),
            planes(4, 4, 11),
            pltpu.VMEM((4, 53, OWN_X, OWN_Y), jnp.float32),
            planes(2, 16),
            pltpu.VMEM((5, 64, OWN_Y), jnp.float32),
            pltpu.VMEM((5, 128, OWN_Y), jnp.float32),
            pltpu.VMEM((10, 128, OWN_Y), jnp.float32),
            pltpu.VMEM((10, 256, OWN_Y), jnp.float32),
        ],
        compiler_params=limit,
        name="moments",
    )(edge, tall, high, from_left, from_right)
    gram = spread_sum(spread_sum(gram, "gx"), "gy")
    return pl.pallas_call(
        finish_kernel,
        out_shape=shaped(8, OWN_X, OWN_Y),
        in_specs=[VMEM] * 2,
        out_specs=VMEM,
        compiler_params=limit,
        name="finish",
    )(gram, mixes)


def solution(mesh):
    in_specs = (
        P(None, None, "gx", "gy"),
        P("gx", "gy"),
        P("gx", "gy"),
        P("gx", "gy"),
        P("gx", "gy"),
        P("gx", "gy"),
        P(None, "gx", "gy"),
    )
    out_specs = P(None, "gx", "gy")
    return jax.shard_map(body, mesh=mesh, in_specs=in_specs, out_specs=out_specs, check_vma=False)
```

```python
import functools

import jax
import jax.numpy as jnp
from jax import lax
from jax.experimental import pallas as pl
from jax.experimental.pallas import tpu as pltpu
from jax.sharding import PartitionSpec as P

MASS_TERM = 0.1
STRAIN_OFFSET = 0.01
PRECISE = lax.Precision.HIGHEST

ROWS = 16
LANES = 256
OWN_X = 8
OWN_Y = 128
LOW = 4
THICK, MASK, FRIC, OBS, PROBE = 22, 23, 24, 25, 26
PLANES = 40


def dot(left, right, dims=((1,), (0,))):
    return lax.dot_general(
        left, right, (dims, ((), ())), precision=PRECISE, preferred_element_type=jnp.float32
    )


def shift(plane, step, axis):
    size = plane.shape[axis]
    return pltpu.roll(plane, (-step) % size, axis)


def pack_kernel(vel, thick, logf, obs, mask, ground, probes, own, up, down, land, land_int, sems):
    moves = [
        (vel.at[0], own.at[pl.ds(0, 11)]),
        (vel.at[1], own.at[pl.ds(11, 11)]),
        (thick, own.at[THICK]),
        (probes, own.at[pl.ds(PROBE, 8)]),
        (logf, land.at[0]),
        (obs, land.at[1]),
        (mask, land_int.at[0]),
        (ground, land_int.at[1]),
    ]
    copies = [pltpu.make_async_copy(src, dst, sems.at[k]) for k, (src, dst) in enumerate(moves)]
    for copy in copies:
        copy.start()
    for copy in copies:
        copy.wait()
    m = land_int[0].astype(jnp.float32)
    own[MASK] = m
    own[FRIC] = m * land_int[1].astype(jnp.float32) * jnp.exp(land[0])
    own[OBS] = land[1] * m
    for k in range(34):
        up[pl.ds(LOW * k, LOW), :] = own[k, OWN_X - LOW :, :]
        down[pl.ds(LOW * k, LOW), :] = own[k, :LOW, :]
        if k < 22:
            down[pl.ds(LOW * PLANES + k, 1), :] = own[k, LOW : LOW + 1, :]


def strip_kernel(edge, own, low, high, tall, left, right):
    keep_low = jnp.where(edge[0] == 0, 0.0, 1.0)
    keep_high = jnp.where(edge[1] == 0, 0.0, 1.0)
    for k in range(34):
        tall[k, 0:OWN_X, :] = own[k]
        tall[k, OWN_X : OWN_X + LOW, :] = high[pl.ds(LOW * k, LOW), :] * keep_high
        tall[k, ROWS - LOW : ROWS, :] = low[pl.ds(LOW * k, LOW), :] * keep_low
    for k in range(34, PLANES):
        tall[k] = jnp.zeros((ROWS, OWN_Y), jnp.float32)
    for b in range(PLANES // 8):
        turned = tall[8 * b : 8 * b + 8].reshape(8 * ROWS, OWN_Y).T
        left[:, OWN_Y * b : OWN_Y * (b + 1)] = turned[0:8]
        right[:, OWN_Y * b : OWN_Y * (b + 1)] = turned[OWN_Y - 8 : OWN_Y]


def moments_kernel(
    edge, tall, high, from_left, from_right, gram, mixes,
    full, row12, mu, kx, kxm, ky, kym, kz, inv, ratio, resp, phi, gam, wts, basis,
    lhs8, rhs8, lhs16, rhs16,
):
    keep_left = jnp.where(edge[2] == 0, 0.0, 1.0)
    keep_right = jnp.where(edge[3] == 0, 0.0, 1.0)
    keep_high = jnp.where(edge[1] == 0, 0.0, 1.0)
    gap = jnp.zeros((OWN_Y - 16, OWN_Y), jnp.float32)
    for b in range(PLANES // 8):
        cols = slice(OWN_Y * b, OWN_Y * (b + 1))
        block = jnp.concatenate(
            [from_right[:, cols] * keep_right, gap, from_left[:, cols] * keep_left], axis=0
        )
        full[8 * b : 8 * b + 8, :, OWN_Y:] = block.T.reshape(8, ROWS, OWN_Y)
        full[8 * b : 8 * b + 8, :, :OWN_Y] = tall[8 * b : 8 * b + 8]
    row12[...] = high[pl.ds(LOW * PLANES, 24), :] * keep_high

    m = full[MASK]
    icy = m > 0.5
    thick = jnp.where(icy, full[THICK], 1.0)
    steep = 10.0 / thick
    half_steep = 0.5 * steep
    steep2 = 0.5 * steep * steep
    mm_x = 0.5 * (m * shift(m, 1, 0))
    mm_y = 0.5 * (m * shift(m, 1, 1))
    fric = full[FRIC]
    base = MASS_TERM * m + (1.0 - m)
    last = lax.broadcasted_iota(jnp.int32, (ROWS, LANES), 0) == OWN_X + LOW - 1

    for l in range(11):
        grads = []
        for c in range(2):
            w = full[11 * c + l]
            beyond = jnp.concatenate(
                [row12[11 * c + l : 11 * c + l + 1, :], jnp.zeros((1, OWN_Y), jnp.float32)], axis=1
            )
            ahead = jnp.where(last, jnp.broadcast_to(beyond, (ROWS, LANES)), shift(w, 1, 0))
            gx = 0.5 * (ahead - shift(w, -1, 0))
            gy = 0.5 * (shift(w, 1, 1) - shift(w, -1, 1))
            gz = (full[11 * c + min(l + 1, 10)] - full[11 * c + max(l - 1, 0)]) * half_steep
            grads.append((gx, gy, gz))
        (ux, uy, uz), (vx, vy, vz) = grads
        cross = uy + vx
        e2 = ux * ux + vy * vy + ux * vy + 0.25 * (cross * cross + uz * uz + vz * vz) + STRAIN_OFFSET
        mu[l] = jnp.where(icy, 0.5 * jnp.exp(jnp.log(e2) * (-1.0 / 3.0)), 0.0)

    kz[0] = jnp.zeros((ROWS, LANES), jnp.float32)
    kz[11] = jnp.zeros((ROWS, LANES), jnp.float32)
    for l in range(11):
        here = mu[l]
        ex = (here + shift(here, 1, 0)) * mm_x
        ey = (here + shift(here, 1, 1)) * mm_y
        kx[l] = ex
        ky[l] = ey
        kxm[l] = shift(ex, -1, 0)
        kym[l] = shift(ey, -1, 1)
        if l < 10:
            kz[l + 1] = (here + mu[l + 1]) * steep2

    last_ratio, carry, top = [None] * 2, [None] * 2, [None] * 2
    for l in range(11):
        side_x, side_y = kx[l] + kxm[l], ky[l] + kym[l]
        rest = base + kz[l] + kz[l + 1]
        for c in range(2):
            main = (4.0 * side_x + side_y if c == 0 else side_x + 4.0 * side_y) + rest
            main = main + fric if l == 0 else main - kz[l] * last_ratio[c]
            recip = 1.0 / main
            last_ratio[c] = kz[l + 1] * recip
            inv[c, l] = recip
            ratio[c, l] = last_ratio[c]
            carry[c] = (fric * full[11 * c] if l == 0 else kz[l] * carry[c]) * recip
            resp[c, l] = carry[c]
            if l == 10:
                top[c] = recip
                resp[2 + c, 10] = recip
    for l in range(9, -1, -1):
        for c in range(2):
            step = ratio[c, l]
            carry[c] = resp[c, l] + step * carry[c]
            resp[c, l] = carry[c]
            top[c] = step * top[c]
            resp[2 + c, l] = top[c]

    def one_kind(kc, _):
        c = lax.rem(kc, 2)
        a = jnp.where(c == 0, 4.0, 1.0)
        b = 5.0 - a
        carry = [None] * 4
        n1 = [None] * 4
        for l in range(11):
            e = resp[kc, l]
            parts = [
                a * (kx[l] * shift(e, 1, 0)),
                a * (kxm[l] * shift(e, -1, 0)),
                b * (ky[l] * shift(e, 1, 1)),
                b * (kym[l] * shift(e, -1, 1)),
            ]
            scale = inv[c, l]
            for s in range(4):
                phi[s, l] = parts[s][:OWN_X, :OWN_Y]
                total = parts[s] if l == 0 else parts[s] + kz[l] * carry[s]
                carry[s] = total * scale
                gam[kc, s, l] = carry[s]
            for s in range(4):
                term = (e * parts[s])[:OWN_X, :OWN_Y]
                n1[s] = term if l == 0 else n1[s] + term
        for s in range(4):
            wts[kc, 1 + s] = n1[s]
        for l in range(9, -1, -1):
            step = ratio[c, l]
            for s in range(4):
                carry[s] = gam[kc, s, l] + step * carry[s]
                gam[kc, s, l] = carry[s]
        own = (slice(0, OWN_X), slice(0, OWN_Y))
        acc = [None] * 16
        for l in range(11):
            f = [phi[s, l] for s in range(4)]
            g = [gam[kc, s, l][own] for s in range(4)]
            for s in range(4):
                for t in range(s, 4):
                    term = f[s] * g[t]
                    acc[4 * s + t] = term if l == 0 else acc[4 * s + t] + term
        for s in range(4):
            for t in range(4):
                wts[kc, 5 + 4 * s + t] = acc[4 * min(s, t) + max(s, t)]
        for way in range(2):
            acc = [None] * 16
            for l in range(11):
                edge_k = kx[l][own] * a if way == 0 else ky[l][own] * b
                g = [gam[kc, s, l][own] * edge_k for s in range(4)]
                if way == 0:
                    h = [shift(gam[kc, s, l, :, :OWN_Y], 1, 0)[:OWN_X] for s in range(4)]
                else:
                    h = [shift(gam[kc, s, l, :OWN_X, :], 1, 1)[:, :OWN_Y] for s in range(4)]
                for s in range(4):
                    for t in range(4):
                        term = g[s] * h[t]
                        acc[4 * s + t] = term if l == 0 else acc[4 * s + t] + term
            for s in range(16):
                wts[kc, 21 + 16 * way + s] = acc[s]
        return 0

    lax.fori_loop(0, 4, one_kind, 0)
    own = (slice(0, OWN_X), slice(0, OWN_Y))
    for c in range(2):
        source = (fric * full[11 * c])[own]
        wts[c, 0] = source * resp[c, 0][own]
        wts[2 + c, 0] = resp[2 + c, 10][own]
    for k in range(53):
        wts[0, k] = wts[0, k] + wts[1, k]

    obs = full[OBS]

    def one_probe(a, _):
        p = full[PROBE + a]
        near = [shift(p, 1, 0), shift(p, -1, 0), shift(p, 1, 1), shift(p, -1, 1)]
        for c in range(2):
            basis[c, a] = obs * resp[c, 10] * p
            total = gam[c, 0, 10] * near[0]
            for s in range(1, 4):
                total = total + gam[c, s, 10] * near[s]
            basis[c, 8 + a] = obs * total
        return 0

    lax.fori_loop(0, 8, one_probe, 0)

    def shifted(plane):
        mid = plane[:, :OWN_Y]
        yp = shift(plane, 1, 1)
        ym = shift(plane, -1, 1)[:, :OWN_Y]
        y2 = shift(yp[:OWN_X], 1, 1)[:, :OWN_Y]
        yp = yp[:, :OWN_Y]
        p00 = mid[:OWN_X]
        pxp, pxm, px2 = (shift(mid, d, 0)[:OWN_X] for d in (1, -1, 2))
        pyp, pxpyp, pxmyp = yp[:OWN_X], shift(yp, 1, 0)[:OWN_X], shift(yp, -1, 0)[:OWN_X]
        pym, pxpym = ym[:OWN_X], shift(ym, 1, 0)[:OWN_X]
        return p00, [pxp, pxm, pyp, pym], [px2, p00, pxpyp, pxpym], [pxpyp, pxmyp, y2, p00]

    def fill(kc, b, plane, many, lhs, rhs, first):
        p00, near, past_x, past_y = shifted(plane)
        here = pl.ds(b, OWN_X, stride=many)
        one = pl.ds(b, OWN_X, stride=2 * many)
        two = pl.ds(many + b, OWN_X, stride=2 * many)
        for t in range(4):
            second = wts[kc, 5 + 4 * t] * near[0]
            for s in range(1, 4):
                second = second + wts[kc, 5 + 4 * t + s] * near[s]
            third = wts[kc, 21 + 4 * t] * past_x[0] + wts[kc, 37 + 4 * t] * past_y[0]
            for s in range(1, 4):
                third = third + wts[kc, 21 + 4 * t + s] * past_x[s]
                third = third + wts[kc, 37 + 4 * t + s] * past_y[s]
            lhs[first + t, here, :] = near[t]
            rhs[first + t, one, :] = second
            rhs[first + t, two, :] = third
        lhs[first + 4, here, :] = p00
        rhs[first + 4, one, :] = wts[kc, 0] * p00
        side = wts[kc, 1] * near[0]
        for s in range(1, 4):
            side = side + wts[kc, 1 + s] * near[s]
        rhs[first + 4, two, :] = side
        return p00, near

    def side_by_side(ref, which):
        return jnp.concatenate([ref[k] for k in which], axis=1)

    def fold(lhs, rhs, which, many):
        product = dot(side_by_side(lhs, which), side_by_side(rhs, which), ((1,), (1,)))
        row, col = places(OWN_X * many, 2 * OWN_X * many)
        product = jnp.where(row // many == col // (2 * many), product, 0.0)
        total = jnp.sum(product.reshape(OWN_X, many, 2 * OWN_X * many), axis=0)
        if many == 16:
            total = total[:, :128] + total[:, 128:]
        step = 64
        while step >= 2 * many:
            total = total + pltpu.roll(total, step, 1)
            step //= 2
        return total

    def fill_probe(pair, _):
        for b in (2 * pair, 2 * pair + 1):
            fill(0, b, full[PROBE + b], 8, lhs8, rhs8, 0)
        return 0

    lax.fori_loop(0, 4, fill_probe, 0)

    weights = [(fric * full[11 * c])[own] for c in range(2)]

    def fill_basis(pair, _):
        for b in (2 * pair, 2 * pair + 1):
            one = two = None
            for c in range(2):
                p00, near = fill(2 + c, b, basis[c, b], 16, lhs16, rhs16, 5 * c)
                here = resp[2 + c, 0, :OWN_X, :OWN_Y] * p00
                there = gam[2 + c, 0, 0, :OWN_X, :OWN_Y] * near[0]
                for s in range(1, 4):
                    there = there + gam[2 + c, s, 0, :OWN_X, :OWN_Y] * near[s]
                one = weights[c] * here if c == 0 else one + weights[c] * here
                two = weights[c] * there if c == 0 else two + weights[c] * there
            mixes[b] = one
            mixes[16 + b] = two
        return 0

    lax.fori_loop(0, 8, fill_basis, 0)

    ends8, sides8 = fold(lhs8, rhs8, (4,), 8), fold(lhs8, rhs8, (0, 1, 2, 3), 8)
    ends16, sides16 = fold(lhs16, rhs16, (4, 9), 16), fold(lhs16, rhs16, (0, 1, 2, 3, 5, 6, 7, 8), 16)

    def woven(ends, many):
        row, col = places(many, 128)
        other = pltpu.roll(ends, 128 - many, 1)
        line = jnp.sum(jnp.where(row == col, other, 0.0), axis=1, keepdims=True)
        return jnp.where(row <= col, ends, other), line

    square16, line16 = woven(ends16, 16)
    square8, line8 = woven(ends8, 8)
    _, col = places(16, 128)
    tall16 = jnp.where(col < 16, square16, pltpu.roll(sides16, 16, 1))
    _, col = places(8, 128)
    message = jnp.where(col < 48, tall16[:8], pltpu.roll(tall16[8:], 48, 1))
    message = jnp.where(col < 96, message, pltpu.roll(square8, 96, 1))
    message = jnp.where(col < 104, message, pltpu.roll(sides8, 104, 1))
    message = jnp.where(col < 120, message, line16[:8])
    message = jnp.where(col < 121, message, line16[8:])
    message = jnp.where(col < 122, message, line8)
    gram[...] = jnp.where(col < 123, message, 0.0)


def places(rows, cols):
    return lax.broadcasted_iota(jnp.int32, (rows, cols), 0), lax.broadcasted_iota(jnp.int32, (rows, cols), 1)


def turned(square):
    row, col = places(square.shape[0], square.shape[0])
    return dot(jnp.where(row == col, 1.0, 0.0), square, ((1,), (1,)))


def parted(packed, line):
    size = packed.shape[0]
    row, col = places(size, size)
    square = packed[:, :size]
    other = turned(square)
    half = packed[:, 2 * size : 3 * size]
    return (
        jnp.where(row <= col, square, other),
        jnp.where(row > col, square, jnp.where(row == col, line, other)),
        packed[:, size : 2 * size],
        half + turned(half),
    )


def krylov_solve(moments, sides):
    m0, m1, m2, m3 = moments
    low = m1 - m2
    square = jnp.concatenate(
        [jnp.concatenate([m0 - m1, low], axis=1), jnp.concatenate([low, m2 - m3], axis=1)], axis=0
    )
    row, col = places(16, 16)
    kept = jnp.where(row == col, square, 0.0)
    tall, wide = jnp.sum(kept, axis=1, keepdims=True), jnp.sum(kept, axis=0, keepdims=True)
    tall = jnp.where(tall > 0.0, lax.rsqrt(tall), 0.0)
    wide = jnp.where(wide > 0.0, lax.rsqrt(wide), 0.0)
    square = jnp.where((row == col) & (tall == 0.0), 1.0, square * tall * wide)
    system = jnp.concatenate([square, jnp.concatenate(sides, axis=0) * tall], axis=1)
    row, _ = places(*system.shape)
    for k in range(0, 16, 2):
        one, two = system[k : k + 1, :], system[k + 1 : k + 2, :]
        left = jnp.broadcast_to(system[:, k : k + 1], system.shape)
        right = jnp.broadcast_to(system[:, k + 1 : k + 2], system.shape)
        p, q = left[k : k + 1, :], right[k : k + 1, :]
        r, t = left[k + 1 : k + 2, :], right[k + 1 : k + 2, :]
        scale = 1.0 / (p * t - q * r)
        first = (t * one - q * two) * scale
        second = (p * two - r * one) * scale
        rest = system - left * first - right * second
        system = jnp.where(row == k, first, jnp.where(row == k + 1, second, rest))
    return system[:, 16:] * tall


def raised(coef):
    rows, cols = coef.shape
    tall = jnp.broadcast_to(coef[:, None, :], (rows, OWN_X, cols)).reshape(rows * OWN_X, cols)
    row, col = places(rows * OWN_X, cols)
    return jnp.where(row % OWN_X == col % OWN_X, tall, 0.0)


def finish_kernel(gram, mixes, out):
    tn = ((0,), (0,))
    row, col = places(8, 64)
    repeat = jnp.where(col // 8 == row, 1.0, 0.0)
    first = parted(gram[:, 96:120], gram[:, 122:123])
    wide = krylov_solve(first, [dot(first[0], repeat), dot(first[1], repeat)])
    row, col = places(64, 8)
    mix = dot(wide, jnp.where(row == 8 * col, 1.0, 0.0))
    adjoint = parted(
        jnp.concatenate([gram[:, 0:48], gram[:, 48:96]], axis=0),
        jnp.concatenate([gram[:, 120:121], gram[:, 121:122]], axis=0),
    )
    half = dot(mix, jnp.concatenate(adjoint, axis=1), tn)
    halves = [half[:, 16 * k : 16 * k + 16] for k in range(4)]
    second = [dot(part, mix) for part in halves]
    coef = krylov_solve(second, [dot(halves[0], wide), dot(halves[1], wide)])
    spread = raised(wide)
    flat = jnp.concatenate([dot(spread, mixes[16 * k : 16 * k + 16].reshape(128, OWN_Y), tn) for k in range(2)], axis=0)
    out[...] = dot(raised(coef), flat, tn).reshape(8, OWN_X, OWN_Y)


VMEM = pl.BlockSpec(memory_space=pltpu.VMEM)
SMEM = pl.BlockSpec(memory_space=pltpu.SMEM)


def shaped(*dims):
    return jax.ShapeDtypeStruct(dims, jnp.float32)


def spread_sum(values, axis):
    count = lax.axis_size(axis)
    copies = jnp.broadcast_to(values, (count,) + values.shape)
    return jnp.sum(lax.all_to_all(copies, axis, 0, 0), axis=0)


def ring(values, axis, step):
    count = lax.axis_size(axis)
    return lax.ppermute(values, axis, [(i, (i + step) % count) for i in range(count)])


def body(velocity, thickness, log_friction, obs_weight, ice_mask, grounded, probes):
    at_x, at_y = lax.axis_index("gx"), lax.axis_index("gy")
    edge = jnp.stack(
        [at_x, lax.axis_size("gx") - 1 - at_x, at_y, lax.axis_size("gy") - 1 - at_y]
    ).astype(jnp.int32)
    limit = pltpu.CompilerParams(vmem_limit_bytes=48 * 1024 * 1024)
    args = (velocity, thickness, log_friction, obs_weight, ice_mask, grounded, probes)
    own, up, down = pl.pallas_call(
        pack_kernel,
        out_shape=(shaped(34, OWN_X, OWN_Y), shaped(LOW * PLANES, OWN_Y), shaped(LOW * PLANES + 24, OWN_Y)),
        in_specs=[pl.BlockSpec(memory_space=pltpu.HBM)] * 7,
        out_specs=(VMEM,) * 3,
        scratch_shapes=[
            pltpu.VMEM((2, OWN_X, OWN_Y), jnp.float32),
            pltpu.VMEM((2, OWN_X, OWN_Y), jnp.int32),
            pltpu.SemaphoreType.DMA((8,)),
        ],
        compiler_params=limit,
        name="pack",
    )(*[pltpu.with_memory_space_constraint(value, pltpu.HBM) for value in args])
    low = ring(up, "gx", 1)
    high = ring(down, "gx", -1)
    tall, left, right = pl.pallas_call(
        strip_kernel,
        out_shape=(shaped(PLANES, ROWS, OWN_Y), shaped(8, OWN_Y * PLANES // 8), shaped(8, OWN_Y * PLANES // 8)),
        in_specs=[SMEM] + [VMEM] * 3,
        out_specs=(VMEM,) * 3,
        compiler_params=limit,
        name="strip",
    )(edge, own, low, high)
    from_left = ring(right, "gy", 1)
    from_right = ring(left, "gy", -1)

    def planes(*lead):
        return pltpu.VMEM(lead + (ROWS, LANES), jnp.float32)

    gram, mixes = pl.pallas_call(
        moments_kernel,
        out_shape=(shaped(8, 128), shaped(32, OWN_X, OWN_Y)),
        in_specs=[SMEM] + [VMEM] * 4,
        out_specs=(VMEM,) * 2,
        scratch_shapes=[
            planes(PLANES),
            pltpu.VMEM((24, OWN_Y), jnp.float32),
            planes(11),
            planes(11),
            planes(11),
            planes(11),
            planes(11),
            planes(12),
            planes(2, 11),
            planes(2, 11),
            planes(4, 11),
            pltpu.VMEM((4, 11, OWN_X, OWN_Y), jnp.float32),
            planes(4, 4, 11),
            pltpu.VMEM((4, 53, OWN_X, OWN_Y), jnp.float32),
            planes(2, 16),
            pltpu.VMEM((5, 64, OWN_Y), jnp.float32),
            pltpu.VMEM((5, 128, OWN_Y), jnp.float32),
            pltpu.VMEM((10, 128, OWN_Y), jnp.float32),
            pltpu.VMEM((10, 256, OWN_Y), jnp.float32),
        ],
        compiler_params=limit,
        name="moments",
    )(edge, tall, high, from_left, from_right)
    gram = spread_sum(spread_sum(gram, "gx"), "gy")
    return pl.pallas_call(
        finish_kernel,
        out_shape=shaped(8, OWN_X, OWN_Y),
        in_specs=[VMEM] * 2,
        out_specs=VMEM,
        compiler_params=limit,
        name="finish",
    )(gram, mixes)


def solution(mesh):
    in_specs = (
        P(None, None, "gx", "gy"),
        P("gx", "gy"),
        P("gx", "gy"),
        P("gx", "gy"),
        P("gx", "gy"),
        P("gx", "gy"),
        P(None, "gx", "gy"),
    )
    out_specs = P(None, "gx", "gy")
    return jax.shard_map(body, mesh=mesh, in_specs=in_specs, out_specs=out_specs, check_vma=False)
```

```python
import functools

import jax
import jax.numpy as jnp
from jax import lax
from jax.experimental import pallas as pl
from jax.experimental.pallas import tpu as pltpu
from jax.sharding import PartitionSpec as P

MASS_TERM = 0.1
STRAIN_OFFSET = 0.01
PRECISE = lax.Precision.HIGHEST

ROWS = 16
LANES = 256
OWN_X = 8
OWN_Y = 128
LOW = 4
THICK, MASK, FRIC, OBS, PROBE = 22, 23, 24, 25, 26
PLANES = 40


def dot(left, right, dims=((1,), (0,))):
    return lax.dot_general(
        left, right, (dims, ((), ())), precision=PRECISE, preferred_element_type=jnp.float32
    )


def shift(plane, step, axis):
    size = plane.shape[axis]
    return pltpu.roll(plane, (-step) % size, axis)


def pack_kernel(vel, thick, logf, obs, mask, ground, probes, own, up, down, land, land_int, sems):
    moves = [
        (vel.at[0], own.at[pl.ds(0, 11)]),
        (vel.at[1], own.at[pl.ds(11, 11)]),
        (thick, own.at[THICK]),
        (probes, own.at[pl.ds(PROBE, 8)]),
        (logf, land.at[0]),
        (obs, land.at[1]),
        (mask, land_int.at[0]),
        (ground, land_int.at[1]),
    ]
    copies = [pltpu.make_async_copy(src, dst, sems.at[k]) for k, (src, dst) in enumerate(moves)]
    for copy in copies:
        copy.start()
    for copy in copies:
        copy.wait()
    m = land_int[0].astype(jnp.float32)
    own[MASK] = m
    own[FRIC] = m * land_int[1].astype(jnp.float32) * jnp.exp(land[0])
    own[OBS] = land[1] * m
    for k in range(34):
        up[pl.ds(LOW * k, LOW), :] = own[k, OWN_X - LOW :, :]
        down[pl.ds(LOW * k, LOW), :] = own[k, :LOW, :]
        if k < 22:
            down[pl.ds(LOW * PLANES + k, 1), :] = own[k, LOW : LOW + 1, :]


def strip_kernel(edge, own, low, high, tall, left, right):
    keep_low = jnp.where(edge[0] == 0, 0.0, 1.0)
    keep_high = jnp.where(edge[1] == 0, 0.0, 1.0)
    for k in range(34):
        tall[k, 0:OWN_X, :] = own[k]
        tall[k, OWN_X : OWN_X + LOW, :] = high[pl.ds(LOW * k, LOW), :] * keep_high
        tall[k, ROWS - LOW : ROWS, :] = low[pl.ds(LOW * k, LOW), :] * keep_low
    for k in range(34, PLANES):
        tall[k] = jnp.zeros((ROWS, OWN_Y), jnp.float32)
    for b in range(PLANES // 8):
        turned = tall[8 * b : 8 * b + 8].reshape(8 * ROWS, OWN_Y).T
        left[:, OWN_Y * b : OWN_Y * (b + 1)] = turned[0:8]
        right[:, OWN_Y * b : OWN_Y * (b + 1)] = turned[OWN_Y - 8 : OWN_Y]


def moments_kernel(
    edge, tall, high, from_left, from_right, gram, mixes,
    full, row12, mu, kx, kxm, ky, kym, kz, inv, ratio, resp, phi, gam, wts, basis,
    lhs8, rhs8, lhs16, rhs16,
):
    keep_left = jnp.where(edge[2] == 0, 0.0, 1.0)
    keep_right = jnp.where(edge[3] == 0, 0.0, 1.0)
    keep_high = jnp.where(edge[1] == 0, 0.0, 1.0)
    gap = jnp.zeros((OWN_Y - 16, OWN_Y), jnp.float32)
    for b in range(PLANES // 8):
        cols = slice(OWN_Y * b, OWN_Y * (b + 1))
        block = jnp.concatenate(
            [from_right[:, cols] * keep_right, gap, from_left[:, cols] * keep_left], axis=0
        )
        full[8 * b : 8 * b + 8, :, OWN_Y:] = block.T.reshape(8, ROWS, OWN_Y)
        full[8 * b : 8 * b + 8, :, :OWN_Y] = tall[8 * b : 8 * b + 8]
    row12[...] = high[pl.ds(LOW * PLANES, 24), :] * keep_high

    m = full[MASK]
    icy = m > 0.5
    thick = jnp.where(icy, full[THICK], 1.0)
    steep = 10.0 / thick
    half_steep = 0.5 * steep
    steep2 = 0.5 * steep * steep
    mm_x = 0.5 * (m * shift(m, 1, 0))
    mm_y = 0.5 * (m * shift(m, 1, 1))
    fric = full[FRIC]
    base = MASS_TERM * m + (1.0 - m)
    last = lax.broadcasted_iota(jnp.int32, (ROWS, LANES), 0) == OWN_X + LOW - 1

    for l in range(11):
        grads = []
        for c in range(2):
            w = full[11 * c + l]
            beyond = jnp.concatenate(
                [row12[11 * c + l : 11 * c + l + 1, :], jnp.zeros((1, OWN_Y), jnp.float32)], axis=1
            )
            ahead = jnp.where(last, jnp.broadcast_to(beyond, (ROWS, LANES)), shift(w, 1, 0))
            gx = 0.5 * (ahead - shift(w, -1, 0))
            gy = 0.5 * (shift(w, 1, 1) - shift(w, -1, 1))
            gz = (full[11 * c + min(l + 1, 10)] - full[11 * c + max(l - 1, 0)]) * half_steep
            grads.append((gx, gy, gz))
        (ux, uy, uz), (vx, vy, vz) = grads
        cross = uy + vx
        e2 = ux * ux + vy * vy + ux * vy + 0.25 * (cross * cross + uz * uz + vz * vz) + STRAIN_OFFSET
        mu[l] = jnp.where(icy, 0.5 * jnp.exp(jnp.log(e2) * (-1.0 / 3.0)), 0.0)

    kz[0] = jnp.zeros((ROWS, LANES), jnp.float32)
    kz[11] = jnp.zeros((ROWS, LANES), jnp.float32)
    for l in range(11):
        here = mu[l]
        ex = (here + shift(here, 1, 0)) * mm_x
        ey = (here + shift(here, 1, 1)) * mm_y
        kx[l] = ex
        ky[l] = ey
        kxm[l] = shift(ex, -1, 0)
        kym[l] = shift(ey, -1, 1)
        if l < 10:
            kz[l + 1] = (here + mu[l + 1]) * steep2

    share, carry, top = [None] * 2, [None] * 2, [None] * 2
    for l in range(11):
        side_x, side_y = kx[l] + kxm[l], ky[l] + kym[l]
        rest = base + fric if l == 0 else base
        for c in range(2):
            excess = (4.0 * side_x + side_y if c == 0 else side_x + 4.0 * side_y) + rest
            if l > 0:
                excess = excess + kz[l] * share[c]
            recip = 1.0 / (excess + kz[l + 1])
            share[c] = excess * recip
            inv[c, l] = recip
            ratio[c, l] = kz[l + 1] * recip
            carry[c] = (fric * full[11 * c] if l == 0 else kz[l] * carry[c]) * recip
            resp[c, l] = carry[c]
            if l == 10:
                top[c] = recip
                resp[2 + c, 10] = recip
    for l in range(9, -1, -1):
        for c in range(2):
            step = ratio[c, l]
            carry[c] = resp[c, l] + step * carry[c]
            resp[c, l] = carry[c]
            top[c] = step * top[c]
            resp[2 + c, l] = top[c]

    def one_kind(kc, _):
        c = lax.rem(kc, 2)
        a = jnp.where(c == 0, 4.0, 1.0)
        b = 5.0 - a
        carry = [None] * 4
        n1 = [None] * 4
        for l in range(11):
            e = resp[kc, l]
            parts = [
                a * (kx[l] * shift(e, 1, 0)),
                a * (kxm[l] * shift(e, -1, 0)),
                b * (ky[l] * shift(e, 1, 1)),
                b * (kym[l] * shift(e, -1, 1)),
            ]
            scale = inv[c, l]
            for s in range(4):
                phi[s, l] = parts[s][:OWN_X, :OWN_Y]
                total = parts[s] if l == 0 else parts[s] + kz[l] * carry[s]
                carry[s] = total * scale
                gam[kc, s, l] = carry[s]
            for s in range(4):
                term = (e * parts[s])[:OWN_X, :OWN_Y]
                n1[s] = term if l == 0 else n1[s] + term
        for s in range(4):
            wts[kc, 1 + s] = n1[s]
        for l in range(9, -1, -1):
            step = ratio[c, l]
            for s in range(4):
                carry[s] = gam[kc, s, l] + step * carry[s]
                gam[kc, s, l] = carry[s]
        own = (slice(0, OWN_X), slice(0, OWN_Y))
        acc = [None] * 16
        for l in range(11):
            f = [phi[s, l] for s in range(4)]
            g = [gam[kc, s, l][own] for s in range(4)]
            for s in range(4):
                for t in range(s, 4):
                    term = f[s] * g[t]
                    acc[4 * s + t] = term if l == 0 else acc[4 * s + t] + term
        for s in range(4):
            for t in range(4):
                wts[kc, 5 + 4 * s + t] = acc[4 * min(s, t) + max(s, t)]
        for way in range(2):
            acc = [None] * 16
            for l in range(11):
                edge_k = kx[l][own] * a if way == 0 else ky[l][own] * b
                g = [gam[kc, s, l][own] * edge_k for s in range(4)]
                if way == 0:
                    h = [shift(gam[kc, s, l, :, :OWN_Y], 1, 0)[:OWN_X] for s in range(4)]
                else:
                    h = [shift(gam[kc, s, l, :OWN_X, :], 1, 1)[:, :OWN_Y] for s in range(4)]
                for s in range(4):
                    for t in range(4):
                        term = g[s] * h[t]
                        acc[4 * s + t] = term if l == 0 else acc[4 * s + t] + term
            for s in range(16):
                wts[kc, 21 + 16 * way + s] = acc[s]
        return 0

    lax.fori_loop(0, 4, one_kind, 0)
    own = (slice(0, OWN_X), slice(0, OWN_Y))
    for c in range(2):
        source = (fric * full[11 * c])[own]
        wts[c, 0] = source * resp[c, 0][own]
        wts[2 + c, 0] = resp[2 + c, 10][own]
    for k in range(53):
        wts[0, k] = wts[0, k] + wts[1, k]

    obs = full[OBS]

    def one_probe(a, _):
        p = full[PROBE + a]
        near = [shift(p, 1, 0), shift(p, -1, 0), shift(p, 1, 1), shift(p, -1, 1)]
        for c in range(2):
            basis[c, a] = obs * resp[c, 10] * p
            total = gam[c, 0, 10] * near[0]
            for s in range(1, 4):
                total = total + gam[c, s, 10] * near[s]
            basis[c, 8 + a] = obs * total
        return 0

    lax.fori_loop(0, 8, one_probe, 0)

    def shifted(plane):
        mid = plane[:, :OWN_Y]
        yp = shift(plane, 1, 1)
        ym = shift(plane, -1, 1)[:, :OWN_Y]
        y2 = shift(yp[:OWN_X], 1, 1)[:, :OWN_Y]
        yp = yp[:, :OWN_Y]
        p00 = mid[:OWN_X]
        pxp, pxm, px2 = (shift(mid, d, 0)[:OWN_X] for d in (1, -1, 2))
        pyp, pxpyp, pxmyp = yp[:OWN_X], shift(yp, 1, 0)[:OWN_X], shift(yp, -1, 0)[:OWN_X]
        pym, pxpym = ym[:OWN_X], shift(ym, 1, 0)[:OWN_X]
        return p00, [pxp, pxm, pyp, pym], [px2, p00, pxpyp, pxpym], [pxpyp, pxmyp, y2, p00]

    def fill(kc, b, plane, many, lhs, rhs, first):
        p00, near, past_x, past_y = shifted(plane)
        here = pl.ds(b, OWN_X, stride=many)
        one = pl.ds(b, OWN_X, stride=2 * many)
        two = pl.ds(many + b, OWN_X, stride=2 * many)
        for t in range(4):
            second = wts[kc, 5 + 4 * t] * near[0]
            for s in range(1, 4):
                second = second + wts[kc, 5 + 4 * t + s] * near[s]
            third = wts[kc, 21 + 4 * t] * past_x[0] + wts[kc, 37 + 4 * t] * past_y[0]
            for s in range(1, 4):
                third = third + wts[kc, 21 + 4 * t + s] * past_x[s]
                third = third + wts[kc, 37 + 4 * t + s] * past_y[s]
            lhs[first + t, here, :] = near[t]
            rhs[first + t, one, :] = second
            rhs[first + t, two, :] = third
        lhs[first + 4, here, :] = p00
        rhs[first + 4, one, :] = wts[kc, 0] * p00
        side = wts[kc, 1] * near[0]
        for s in range(1, 4):
            side = side + wts[kc, 1 + s] * near[s]
        rhs[first + 4, two, :] = side
        return p00, near

    def side_by_side(ref, which, rows):
        return jnp.concatenate([ref[k, rows * x : rows * (x + 1)] for k in which for x in range(OWN_X)], axis=1)

    def fold(lhs, rhs, which, many):
        product = dot(side_by_side(lhs, which, many), side_by_side(rhs, which, 2 * many), ((1,), (1,)))
        return jnp.concatenate([product, jnp.zeros((many, 128 - 2 * many), jnp.float32)], axis=1)

    def fill_probe(pair, _):
        for b in (2 * pair, 2 * pair + 1):
            fill(0, b, full[PROBE + b], 8, lhs8, rhs8, 0)
        return 0

    lax.fori_loop(0, 4, fill_probe, 0)

    weights = [(fric * full[11 * c])[own] for c in range(2)]

    def fill_basis(pair, _):
        for b in (2 * pair, 2 * pair + 1):
            one = two = None
            for c in range(2):
                p00, near = fill(2 + c, b, basis[c, b], 16, lhs16, rhs16, 5 * c)
                here = resp[2 + c, 0, :OWN_X, :OWN_Y] * p00
                there = gam[2 + c, 0, 0, :OWN_X, :OWN_Y] * near[0]
                for s in range(1, 4):
                    there = there + gam[2 + c, s, 0, :OWN_X, :OWN_Y] * near[s]
                one = weights[c] * here if c == 0 else one + weights[c] * here
                two = weights[c] * there if c == 0 else two + weights[c] * there
            mixes[b] = one
            mixes[16 + b] = two
        return 0

    lax.fori_loop(0, 8, fill_basis, 0)

    ends8, sides8 = fold(lhs8, rhs8, (4,), 8), fold(lhs8, rhs8, (0, 1, 2, 3), 8)
    ends16, sides16 = fold(lhs16, rhs16, (4, 9), 16), fold(lhs16, rhs16, (0, 1, 2, 3, 5, 6, 7, 8), 16)

    def woven(ends, many):
        row, col = places(many, 128)
        other = pltpu.roll(ends, 128 - many, 1)
        line = jnp.sum(jnp.where(row == col, other, 0.0), axis=1, keepdims=True)
        return jnp.where(row <= col, ends, other), line

    square16, line16 = woven(ends16, 16)
    square8, line8 = woven(ends8, 8)
    _, col = places(16, 128)
    tall16 = jnp.where(col < 16, square16, pltpu.roll(sides16, 16, 1))
    _, col = places(8, 128)
    message = jnp.where(col < 48, tall16[:8], pltpu.roll(tall16[8:], 48, 1))
    message = jnp.where(col < 96, message, pltpu.roll(square8, 96, 1))
    message = jnp.where(col < 104, message, pltpu.roll(sides8, 104, 1))
    message = jnp.where(col < 120, message, line16[:8])
    message = jnp.where(col < 121, message, line16[8:])
    message = jnp.where(col < 122, message, line8)
    gram[...] = jnp.where(col < 123, message, 0.0)


def places(rows, cols):
    return lax.broadcasted_iota(jnp.int32, (rows, cols), 0), lax.broadcasted_iota(jnp.int32, (rows, cols), 1)


def turned(square):
    row, col = places(square.shape[0], square.shape[0])
    return dot(jnp.where(row == col, 1.0, 0.0), square, ((1,), (1,)))


def parted(packed, line):
    size = packed.shape[0]
    row, col = places(size, size)
    square = packed[:, :size]
    other = turned(square)
    half = packed[:, 2 * size : 3 * size]
    return (
        jnp.where(row <= col, square, other),
        jnp.where(row > col, square, jnp.where(row == col, line, other)),
        packed[:, size : 2 * size],
        half + turned(half),
    )


def krylov_solve(moments, sides):
    m0, m1, m2, m3 = moments
    low = m1 - m2
    square = jnp.concatenate(
        [jnp.concatenate([m0 - m1, low], axis=1), jnp.concatenate([low, m2 - m3], axis=1)], axis=0
    )
    row, col = places(16, 16)
    kept = jnp.where(row == col, square, 0.0)
    tall, wide = jnp.sum(kept, axis=1, keepdims=True), jnp.sum(kept, axis=0, keepdims=True)
    tall = jnp.where(tall > 0.0, lax.rsqrt(tall), 0.0)
    wide = jnp.where(wide > 0.0, lax.rsqrt(wide), 0.0)
    square = jnp.where((row == col) & (tall == 0.0), 1.0, square * tall * wide)
    system = jnp.concatenate([square, jnp.concatenate(sides, axis=0) * tall], axis=1)
    row, _ = places(*system.shape)
    for k in range(0, 16, 2):
        one, two = system[k : k + 1, :], system[k + 1 : k + 2, :]
        left = jnp.broadcast_to(system[:, k : k + 1], system.shape)
        right = jnp.broadcast_to(system[:, k + 1 : k + 2], system.shape)
        p, q = left[k : k + 1, :], right[k : k + 1, :]
        r, t = left[k + 1 : k + 2, :], right[k + 1 : k + 2, :]
        scale = 1.0 / (p * t - q * r)
        first = (t * one - q * two) * scale
        second = (p * two - r * one) * scale
        rest = system - left * first - right * second
        system = jnp.where(row == k, first, jnp.where(row == k + 1, second, rest))
    return system[:, 16:] * tall


def raised(coef):
    rows, cols = coef.shape
    tall = jnp.broadcast_to(coef[:, None, :], (rows, OWN_X, cols)).reshape(rows * OWN_X, cols)
    row, col = places(rows * OWN_X, cols)
    return jnp.where(row % OWN_X == col % OWN_X, tall, 0.0)


def finish_kernel(gram, mixes, out):
    tn = ((0,), (0,))
    row, col = places(8, 64)
    repeat = jnp.where(col // 8 == row, 1.0, 0.0)
    first = parted(gram[:, 96:120], gram[:, 122:123])
    wide = krylov_solve(first, [dot(first[0], repeat), dot(first[1], repeat)])
    row, col = places(64, 8)
    mix = dot(wide, jnp.where(row == 8 * col, 1.0, 0.0))
    adjoint = parted(
        jnp.concatenate([gram[:, 0:48], gram[:, 48:96]], axis=0),
        jnp.concatenate([gram[:, 120:121], gram[:, 121:122]], axis=0),
    )
    half = dot(mix, jnp.concatenate(adjoint, axis=1), tn)
    halves = [half[:, 16 * k : 16 * k + 16] for k in range(4)]
    second = [dot(part, mix) for part in halves]
    coef = krylov_solve(second, [dot(halves[0], wide), dot(halves[1], wide)])
    spread = raised(wide)
    flat = jnp.concatenate([dot(spread, mixes[16 * k : 16 * k + 16].reshape(128, OWN_Y), tn) for k in range(2)], axis=0)
    out[...] = dot(raised(coef), flat, tn).reshape(8, OWN_X, OWN_Y)


VMEM = pl.BlockSpec(memory_space=pltpu.VMEM)
SMEM = pl.BlockSpec(memory_space=pltpu.SMEM)


def shaped(*dims):
    return jax.ShapeDtypeStruct(dims, jnp.float32)


def spread_sum(values, axis):
    count = lax.axis_size(axis)
    copies = jnp.broadcast_to(values, (count,) + values.shape)
    return jnp.sum(lax.all_to_all(copies, axis, 0, 0), axis=0)


def ring(values, axis, step):
    count = lax.axis_size(axis)
    return lax.ppermute(values, axis, [(i, (i + step) % count) for i in range(count)])


def body(velocity, thickness, log_friction, obs_weight, ice_mask, grounded, probes):
    at_x, at_y = lax.axis_index("gx"), lax.axis_index("gy")
    edge = jnp.stack(
        [at_x, lax.axis_size("gx") - 1 - at_x, at_y, lax.axis_size("gy") - 1 - at_y]
    ).astype(jnp.int32)
    limit = pltpu.CompilerParams(vmem_limit_bytes=48 * 1024 * 1024)
    args = (velocity, thickness, log_friction, obs_weight, ice_mask, grounded, probes)
    own, up, down = pl.pallas_call(
        pack_kernel,
        out_shape=(shaped(34, OWN_X, OWN_Y), shaped(LOW * PLANES, OWN_Y), shaped(LOW * PLANES + 24, OWN_Y)),
        in_specs=[pl.BlockSpec(memory_space=pltpu.HBM)] * 7,
        out_specs=(VMEM,) * 3,
        scratch_shapes=[
            pltpu.VMEM((2, OWN_X, OWN_Y), jnp.float32),
            pltpu.VMEM((2, OWN_X, OWN_Y), jnp.int32),
            pltpu.SemaphoreType.DMA((8,)),
        ],
        compiler_params=limit,
        name="pack",
    )(*[pltpu.with_memory_space_constraint(value, pltpu.HBM) for value in args])
    low = ring(up, "gx", 1)
    high = ring(down, "gx", -1)
    tall, left, right = pl.pallas_call(
        strip_kernel,
        out_shape=(shaped(PLANES, ROWS, OWN_Y), shaped(8, OWN_Y * PLANES // 8), shaped(8, OWN_Y * PLANES // 8)),
        in_specs=[SMEM] + [VMEM] * 3,
        out_specs=(VMEM,) * 3,
        compiler_params=limit,
        name="strip",
    )(edge, own, low, high)
    from_left = ring(right, "gy", 1)
    from_right = ring(left, "gy", -1)

    def planes(*lead):
        return pltpu.VMEM(lead + (ROWS, LANES), jnp.float32)

    gram, mixes = pl.pallas_call(
        moments_kernel,
        out_shape=(shaped(8, 128), shaped(32, OWN_X, OWN_Y)),
        in_specs=[SMEM] + [VMEM] * 4,
        out_specs=(VMEM,) * 2,
        scratch_shapes=[
            planes(PLANES),
            pltpu.VMEM((24, OWN_Y), jnp.float32),
            planes(11),
            planes(11),
            planes(11),
            planes(11),
            planes(11),
            planes(12),
            planes(2, 11),
            planes(2, 11),
            planes(4, 11),
            pltpu.VMEM((4, 11, OWN_X, OWN_Y), jnp.float32),
            planes(4, 4, 11),
            pltpu.VMEM((4, 53, OWN_X, OWN_Y), jnp.float32),
            planes(2, 16),
            pltpu.VMEM((5, 64, OWN_Y), jnp.float32),
            pltpu.VMEM((5, 128, OWN_Y), jnp.float32),
            pltpu.VMEM((10, 128, OWN_Y), jnp.float32),
            pltpu.VMEM((10, 256, OWN_Y), jnp.float32),
        ],
        compiler_params=limit,
        name="moments",
    )(edge, tall, high, from_left, from_right)
    gram = spread_sum(spread_sum(gram, "gx"), "gy")
    return pl.pallas_call(
        finish_kernel,
        out_shape=shaped(8, OWN_X, OWN_Y),
        in_specs=[VMEM] * 2,
        out_specs=VMEM,
        compiler_params=limit,
        name="finish",
    )(gram, mixes)


def solution(mesh):
    in_specs = (
        P(None, None, "gx", "gy"),
        P("gx", "gy"),
        P("gx", "gy"),
        P("gx", "gy"),
        P("gx", "gy"),
        P("gx", "gy"),
        P(None, "gx", "gy"),
    )
    out_specs = P(None, "gx", "gy")
    return jax.shard_map(body, mesh=mesh, in_specs=in_specs, out_specs=out_specs, check_vma=False)
```

```python
import jax
import jax.numpy as jnp
from jax import lax
from jax.experimental import pallas as pl
from jax.experimental.pallas import tpu as pltpu
from jax.sharding import PartitionSpec as P

MASS_TERM = 0.1
STRAIN_OFFSET = 0.01
PRECISE = lax.Precision.HIGHEST

ROWS = 16
LANES = 256
OWN_X = 8
OWN_Y = 128
LOW = 4
THICK, MASK, FRIC, OBS, PROBE = 22, 23, 24, 25, 26
PLANES = 34


def dot(left, right, dims=((1,), (0,))):
    return lax.dot_general(
        left, right, (dims, ((), ())), precision=PRECISE, preferred_element_type=jnp.float32
    )


def shift(plane, step, axis):
    size = plane.shape[axis]
    return pltpu.roll(plane, (-step) % size, axis)


def pack_kernel(vel, thick, logf, obs, mask, ground, probes, own, up, down, land, land_int, sems):
    moves = [
        (vel.at[0], own.at[pl.ds(0, 11)]),
        (vel.at[1], own.at[pl.ds(11, 11)]),
        (thick, own.at[THICK]),
        (probes, own.at[pl.ds(PROBE, 8)]),
        (logf, land.at[0]),
        (obs, land.at[1]),
        (mask, land_int.at[0]),
        (ground, land_int.at[1]),
    ]
    copies = [pltpu.make_async_copy(src, dst, sems.at[k]) for k, (src, dst) in enumerate(moves)]
    for copy in copies:
        copy.start()
    for copy in copies:
        copy.wait()
    m = land_int[0].astype(jnp.float32)
    own[MASK] = m
    own[FRIC] = m * land_int[1].astype(jnp.float32) * jnp.exp(land[0])
    own[OBS] = land[1] * m
    for k in range(PLANES):
        up[pl.ds(LOW * k, LOW), :] = own[k, OWN_X - LOW :, :]
        down[pl.ds(LOW * k, LOW), :] = own[k, :LOW, :]
        if k < 22:
            down[pl.ds(LOW * PLANES + k, 1), :] = own[k, LOW : LOW + 1, :]


def strip_kernel(edge, own, low, high, tall, left, right):
    keep_low, keep_high = edge[0:1, :], edge[1:2, :]
    for k in range(PLANES):
        tall[k, 0:OWN_X, :] = own[k]
        tall[k, OWN_X : OWN_X + LOW, :] = high[pl.ds(LOW * k, LOW), :] * keep_high
        tall[k, ROWS - LOW : ROWS, :] = low[pl.ds(LOW * k, LOW), :] * keep_low
    group = lax.broadcasted_iota(jnp.int32, (ROWS, OWN_Y), 1) // 8
    for b in range(3):
        first = last = jnp.zeros((ROWS, OWN_Y), jnp.float32)
        for g in range(min(16, PLANES - 16 * b)):
            moved = pltpu.roll(tall[16 * b + g], 8 * g, 1) if g else tall[16 * b]
            first = jnp.where(group == g, moved, first)
            last = jnp.where(group == (g + 15) % 16, moved, last)
        left[b] = first
        right[b] = last


def moments_kernel(
    edge, tall, high, from_left, from_right, gram, mixes,
    full, row12, mu, kx, kxm, ky, kym, kz, inv, ratio, resp, phi, gam, wts, basis,
    lhs8, rhs8, lhs16, rhs16,
):
    keep_high, keep_left, keep_right = edge[1:2, :], edge[2:3, :], edge[3:4, :]
    group = lax.broadcasted_iota(jnp.int32, (ROWS, OWN_Y), 1) // 8
    for b in range(3):
        above, below = from_right[b] * keep_right, from_left[b] * keep_left
        for g in range(min(16, PLANES - 16 * b)):
            k = 16 * b + g
            strips = jnp.where(group == g, above, jnp.where(group == (g + 15) % 16, below, 0.0))
            full[k, :, OWN_Y:] = pltpu.roll(strips, 128 - 8 * g, 1) if g else strips
            full[k, :, :OWN_Y] = tall[k]
    row12[...] = high[pl.ds(LOW * PLANES, 24), :] * keep_high

    m = full[MASK]
    icy = m > 0.5
    thick = jnp.where(icy, full[THICK], 1.0)
    steep = 10.0 / thick
    half_steep = 0.5 * steep
    steep2 = 0.5 * steep * steep
    mm_x = 0.5 * (m * shift(m, 1, 0))
    mm_y = 0.5 * (m * shift(m, 1, 1))
    fric = full[FRIC]
    base = MASS_TERM * m + (1.0 - m)
    last = lax.broadcasted_iota(jnp.int32, (ROWS, LANES), 0) == OWN_X + LOW - 1

    for l in range(11):
        grads = []
        for c in range(2):
            w = full[11 * c + l]
            beyond = jnp.concatenate(
                [row12[11 * c + l : 11 * c + l + 1, :], jnp.zeros((1, OWN_Y), jnp.float32)], axis=1
            )
            ahead = jnp.where(last, jnp.broadcast_to(beyond, (ROWS, LANES)), shift(w, 1, 0))
            gx = 0.5 * (ahead - shift(w, -1, 0))
            gy = 0.5 * (shift(w, 1, 1) - shift(w, -1, 1))
            gz = (full[11 * c + min(l + 1, 10)] - full[11 * c + max(l - 1, 0)]) * half_steep
            grads.append((gx, gy, gz))
        (ux, uy, uz), (vx, vy, vz) = grads
        cross = uy + vx
        e2 = ux * ux + vy * vy + ux * vy + 0.25 * (cross * cross + uz * uz + vz * vz) + STRAIN_OFFSET
        mu[l] = jnp.where(icy, 0.5 * jnp.exp(jnp.log(e2) * (-1.0 / 3.0)), 0.0)

    kz[0] = jnp.zeros((ROWS, LANES), jnp.float32)
    kz[11] = jnp.zeros((ROWS, LANES), jnp.float32)
    for l in range(11):
        here = mu[l]
        ex = (here + shift(here, 1, 0)) * mm_x
        ey = (here + shift(here, 1, 1)) * mm_y
        kx[l] = ex
        ky[l] = ey
        kxm[l] = shift(ex, -1, 0)
        kym[l] = shift(ey, -1, 1)
        if l < 10:
            kz[l + 1] = (here + mu[l + 1]) * steep2

    share, carry, top = [None] * 2, [None] * 2, [None] * 2
    for l in range(11):
        side_x, side_y = kx[l] + kxm[l], ky[l] + kym[l]
        rest = base + fric if l == 0 else base
        for c in range(2):
            excess = (4.0 * side_x + side_y if c == 0 else side_x + 4.0 * side_y) + rest
            if l > 0:
                excess = excess + kz[l] * share[c]
            recip = 1.0 / (excess + kz[l + 1])
            share[c] = excess * recip
            inv[c, l] = recip
            ratio[c, l] = kz[l + 1] * recip
            carry[c] = (fric * full[11 * c] if l == 0 else kz[l] * carry[c]) * recip
            resp[c, l] = carry[c]
            if l == 10:
                top[c] = recip
                resp[2 + c, 10] = recip
    for l in range(9, -1, -1):
        for c in range(2):
            step = ratio[c, l]
            carry[c] = resp[c, l] + step * carry[c]
            resp[c, l] = carry[c]
            top[c] = step * top[c]
            resp[2 + c, l] = top[c]

    def one_kind(kc, _):
        c = lax.rem(kc, 2)
        a = jnp.where(c == 0, 4.0, 1.0)
        b = 5.0 - a
        carry = [None] * 4
        n1 = [None] * 4
        for l in range(11):
            e = resp[kc, l]
            parts = [
                a * (kx[l] * shift(e, 1, 0)),
                a * (kxm[l] * shift(e, -1, 0)),
                b * (ky[l] * shift(e, 1, 1)),
                b * (kym[l] * shift(e, -1, 1)),
            ]
            scale = inv[c, l]
            for s in range(4):
                phi[s, l] = parts[s][:OWN_X, :OWN_Y]
                total = parts[s] if l == 0 else parts[s] + kz[l] * carry[s]
                carry[s] = total * scale
                gam[kc, s, l] = carry[s]
            for s in range(4):
                term = (e * parts[s])[:OWN_X, :OWN_Y]
                n1[s] = term if l == 0 else n1[s] + term
        for s in range(4):
            wts[kc, 1 + s] = n1[s]
        for l in range(9, -1, -1):
            step = ratio[c, l]
            for s in range(4):
                carry[s] = gam[kc, s, l] + step * carry[s]
                gam[kc, s, l] = carry[s]
        own = (slice(0, OWN_X), slice(0, OWN_Y))
        acc = [None] * 16
        for l in range(11):
            f = [phi[s, l] for s in range(4)]
            g = [gam[kc, s, l][own] for s in range(4)]
            for s in range(4):
                for t in range(s, 4):
                    term = f[s] * g[t]
                    acc[4 * s + t] = term if l == 0 else acc[4 * s + t] + term
        for s in range(4):
            for t in range(4):
                wts[kc, 5 + 4 * s + t] = acc[4 * min(s, t) + max(s, t)]
        for way in range(2):
            acc = [None] * 16
            for l in range(11):
                edge_k = kx[l][own] * a if way == 0 else ky[l][own] * b
                g = [gam[kc, s, l][own] * edge_k for s in range(4)]
                if way == 0:
                    h = [shift(gam[kc, s, l, :, :OWN_Y], 1, 0)[:OWN_X] for s in range(4)]
                else:
                    h = [shift(gam[kc, s, l, :OWN_X, :], 1, 1)[:, :OWN_Y] for s in range(4)]
                for s in range(4):
                    for t in range(4):
                        term = g[s] * h[t]
                        acc[4 * s + t] = term if l == 0 else acc[4 * s + t] + term
            for s in range(16):
                wts[kc, 21 + 16 * way + s] = acc[s]
        return 0

    lax.fori_loop(0, 4, one_kind, 0)
    own = (slice(0, OWN_X), slice(0, OWN_Y))
    for c in range(2):
        source = (fric * full[11 * c])[own]
        wts[c, 0] = source * resp[c, 0][own]
        wts[2 + c, 0] = resp[2 + c, 10][own]
    for k in range(53):
        wts[0, k] = wts[0, k] + wts[1, k]

    obs = full[OBS]

    def one_probe(a, _):
        p = full[PROBE + a]
        near = [shift(p, 1, 0), shift(p, -1, 0), shift(p, 1, 1), shift(p, -1, 1)]
        for c in range(2):
            basis[c, a] = obs * resp[c, 10] * p
            total = gam[c, 0, 10] * near[0]
            for s in range(1, 4):
                total = total + gam[c, s, 10] * near[s]
            basis[c, 8 + a] = obs * total
        return 0

    lax.fori_loop(0, 8, one_probe, 0)

    def shifted(plane):
        mid = plane[:, :OWN_Y]
        yp = shift(plane, 1, 1)
        ym = shift(plane, -1, 1)[:, :OWN_Y]
        y2 = shift(yp[:OWN_X], 1, 1)[:, :OWN_Y]
        yp = yp[:, :OWN_Y]
        p00 = mid[:OWN_X]
        pxp, pxm, px2 = (shift(mid, d, 0)[:OWN_X] for d in (1, -1, 2))
        pyp, pxpyp, pxmyp = yp[:OWN_X], shift(yp, 1, 0)[:OWN_X], shift(yp, -1, 0)[:OWN_X]
        pym, pxpym = ym[:OWN_X], shift(ym, 1, 0)[:OWN_X]
        return p00, [pxp, pxm, pyp, pym], [px2, p00, pxpyp, pxpym], [pxpyp, pxmyp, y2, p00]

    def fill(kc, b, plane, many, lhs, rhs, first):
        p00, near, past_x, past_y = shifted(plane)
        here = pl.ds(b, OWN_X, stride=many)
        one = pl.ds(b, OWN_X, stride=2 * many)
        two = pl.ds(many + b, OWN_X, stride=2 * many)
        for t in range(4):
            second = wts[kc, 5 + 4 * t] * near[0]
            for s in range(1, 4):
                second = second + wts[kc, 5 + 4 * t + s] * near[s]
            third = wts[kc, 21 + 4 * t] * past_x[0] + wts[kc, 37 + 4 * t] * past_y[0]
            for s in range(1, 4):
                third = third + wts[kc, 21 + 4 * t + s] * past_x[s]
                third = third + wts[kc, 37 + 4 * t + s] * past_y[s]
            lhs[first + t, here, :] = near[t]
            rhs[first + t, one, :] = second
            rhs[first + t, two, :] = third
        lhs[first + 4, here, :] = p00
        rhs[first + 4, one, :] = wts[kc, 0] * p00
        side = wts[kc, 1] * near[0]
        for s in range(1, 4):
            side = side + wts[kc, 1 + s] * near[s]
        rhs[first + 4, two, :] = side
        return p00, near

    def side_by_side(ref, which, rows):
        return jnp.concatenate([ref[k, rows * x : rows * (x + 1)] for k in which for x in range(OWN_X)], axis=1)

    def fold(lhs, rhs, which, many):
        product = dot(side_by_side(lhs, which, many), side_by_side(rhs, which, 2 * many), ((1,), (1,)))
        return jnp.concatenate([product, jnp.zeros((many, 128 - 2 * many), jnp.float32)], axis=1)

    def fill_probe(pair, _):
        for b in (2 * pair, 2 * pair + 1):
            fill(0, b, full[PROBE + b], 8, lhs8, rhs8, 0)
        return 0

    lax.fori_loop(0, 4, fill_probe, 0)

    weights = [(fric * full[11 * c])[own] for c in range(2)]

    def fill_basis(pair, _):
        for b in (2 * pair, 2 * pair + 1):
            one = two = None
            for c in range(2):
                p00, near = fill(2 + c, b, basis[c, b], 16, lhs16, rhs16, 5 * c)
                here = resp[2 + c, 0, :OWN_X, :OWN_Y] * p00
                there = gam[2 + c, 0, 0, :OWN_X, :OWN_Y] * near[0]
                for s in range(1, 4):
                    there = there + gam[2 + c, s, 0, :OWN_X, :OWN_Y] * near[s]
                one = weights[c] * here if c == 0 else one + weights[c] * here
                two = weights[c] * there if c == 0 else two + weights[c] * there
            mixes[b] = one
            mixes[16 + b] = two
        return 0

    lax.fori_loop(0, 8, fill_basis, 0)

    ends8, sides8 = fold(lhs8, rhs8, (4,), 8), fold(lhs8, rhs8, (0, 1, 2, 3), 8)
    ends16, sides16 = fold(lhs16, rhs16, (4, 9), 16), fold(lhs16, rhs16, (0, 1, 2, 3, 5, 6, 7, 8), 16)

    def woven(ends, many):
        row, col = places(many, 128)
        other = pltpu.roll(ends, 128 - many, 1)
        line = jnp.sum(jnp.where(row == col, other, 0.0), axis=1, keepdims=True)
        return jnp.where(row <= col, ends, other), line

    square16, line16 = woven(ends16, 16)
    square8, line8 = woven(ends8, 8)
    _, col = places(16, 128)
    tall16 = jnp.where(col < 16, square16, pltpu.roll(sides16, 16, 1))
    _, col = places(8, 128)
    message = jnp.where(col < 48, tall16[:8], pltpu.roll(tall16[8:], 48, 1))
    message = jnp.where(col < 96, message, pltpu.roll(square8, 96, 1))
    message = jnp.where(col < 104, message, pltpu.roll(sides8, 104, 1))
    message = jnp.where(col < 120, message, line16[:8])
    message = jnp.where(col < 121, message, line16[8:])
    message = jnp.where(col < 122, message, line8)
    gram[...] = jnp.where(col < 123, message, 0.0)


def places(rows, cols):
    return lax.broadcasted_iota(jnp.int32, (rows, cols), 0), lax.broadcasted_iota(jnp.int32, (rows, cols), 1)


def turned(square):
    row, col = places(square.shape[0], square.shape[0])
    return dot(jnp.where(row == col, 1.0, 0.0), square, ((1,), (1,)))


def parted(packed, line):
    size = packed.shape[0]
    row, col = places(size, size)
    square = packed[:, :size]
    other = turned(square)
    half = packed[:, 2 * size : 3 * size]
    return (
        jnp.where(row <= col, square, other),
        jnp.where(row > col, square, jnp.where(row == col, line, other)),
        packed[:, size : 2 * size],
        half + turned(half),
    )


def krylov_solve(moments, sides):
    m0, m1, m2, m3 = moments
    low = m1 - m2
    square = jnp.concatenate(
        [jnp.concatenate([m0 - m1, low], axis=1), jnp.concatenate([low, m2 - m3], axis=1)], axis=0
    )
    row, col = places(16, 16)
    kept = jnp.where(row == col, square, 0.0)
    tall, wide = jnp.sum(kept, axis=1, keepdims=True), jnp.sum(kept, axis=0, keepdims=True)
    tall = jnp.where(tall > 0.0, lax.rsqrt(tall), 0.0)
    wide = jnp.where(wide > 0.0, lax.rsqrt(wide), 0.0)
    square = jnp.where((row == col) & (tall == 0.0), 1.0, square * tall * wide)
    system = jnp.concatenate([square, jnp.concatenate(sides, axis=0) * tall], axis=1)
    row, _ = places(*system.shape)
    for k in range(0, 16, 2):
        one, two = system[k : k + 1, :], system[k + 1 : k + 2, :]
        left = jnp.broadcast_to(system[:, k : k + 1], system.shape)
        right = jnp.broadcast_to(system[:, k + 1 : k + 2], system.shape)
        p, q = left[k : k + 1, :], right[k : k + 1, :]
        r, t = left[k + 1 : k + 2, :], right[k + 1 : k + 2, :]
        scale = 1.0 / (p * t - q * r)
        first = (t * one - q * two) * scale
        second = (p * two - r * one) * scale
        rest = system - left * first - right * second
        system = jnp.where(row == k, first, jnp.where(row == k + 1, second, rest))
    return system[:, 16:] * tall


def raised(coef):
    rows, cols = coef.shape
    tall = jnp.broadcast_to(coef[:, None, :], (rows, OWN_X, cols)).reshape(rows * OWN_X, cols)
    row, col = places(rows * OWN_X, cols)
    return jnp.where(row % OWN_X == col % OWN_X, tall, 0.0)


def finish_kernel(gram, mixes, out):
    tn = ((0,), (0,))
    row, col = places(8, 64)
    repeat = jnp.where(col // 8 == row, 1.0, 0.0)
    first = parted(gram[:, 96:120], gram[:, 122:123])
    wide = krylov_solve(first, [dot(first[0], repeat), dot(first[1], repeat)])
    row, col = places(64, 8)
    mix = dot(wide, jnp.where(row == 8 * col, 1.0, 0.0))
    adjoint = parted(
        jnp.concatenate([gram[:, 0:48], gram[:, 48:96]], axis=0),
        jnp.concatenate([gram[:, 120:121], gram[:, 121:122]], axis=0),
    )
    half = dot(mix, jnp.concatenate(adjoint, axis=1), tn)
    halves = [half[:, 16 * k : 16 * k + 16] for k in range(4)]
    second = [dot(part, mix) for part in halves]
    coef = krylov_solve(second, [dot(halves[0], wide), dot(halves[1], wide)])
    spread = raised(wide)
    flat = jnp.concatenate([dot(spread, mixes[16 * k : 16 * k + 16].reshape(128, OWN_Y), tn) for k in range(2)], axis=0)
    out[...] = dot(raised(coef), flat, tn).reshape(8, OWN_X, OWN_Y)


VMEM = pl.BlockSpec(memory_space=pltpu.VMEM)


def shaped(*dims):
    return jax.ShapeDtypeStruct(dims, jnp.float32)


def spread_sum(values, axis):
    count = lax.axis_size(axis)
    copies = jnp.broadcast_to(values, (count,) + values.shape)
    return jnp.sum(lax.all_to_all(copies, axis, 0, 0), axis=0)


def ring(values, axis, step):
    count = lax.axis_size(axis)
    return lax.ppermute(values, axis, [(i, (i + step) % count) for i in range(count)])


def body(velocity, thickness, log_friction, obs_weight, ice_mask, grounded, probes):
    at_x, at_y = lax.axis_index("gx"), lax.axis_index("gy")
    row = lax.broadcasted_iota(jnp.int32, (8, OWN_Y), 0)
    ends = [at_x, lax.axis_size("gx") - 1 - at_x, at_y, lax.axis_size("gy") - 1 - at_y]
    edge = jnp.ones((8, OWN_Y), jnp.float32)
    for k, end in enumerate(ends):
        edge = jnp.where((row == k) & (end == 0), 0.0, edge)
    limit = pltpu.CompilerParams(vmem_limit_bytes=48 * 1024 * 1024)
    args = (velocity, thickness, log_friction, obs_weight, ice_mask, grounded, probes)
    own, up, down = pl.pallas_call(
        pack_kernel,
        out_shape=(shaped(PLANES, OWN_X, OWN_Y), shaped(LOW * PLANES, OWN_Y), shaped(LOW * PLANES + 24, OWN_Y)),
        in_specs=[pl.BlockSpec(memory_space=pltpu.HBM)] * 7,
        out_specs=(VMEM,) * 3,
        scratch_shapes=[
            pltpu.VMEM((2, OWN_X, OWN_Y), jnp.float32),
            pltpu.VMEM((2, OWN_X, OWN_Y), jnp.int32),
            pltpu.SemaphoreType.DMA((8,)),
        ],
        compiler_params=limit,
        name="pack",
    )(*[pltpu.with_memory_space_constraint(value, pltpu.HBM) for value in args])
    low = ring(up, "gx", 1)
    high = ring(down, "gx", -1)
    tall, left, right = pl.pallas_call(
        strip_kernel,
        out_shape=(shaped(PLANES, ROWS, OWN_Y), shaped(3, ROWS, OWN_Y), shaped(3, ROWS, OWN_Y)),
        in_specs=[VMEM] * 4,
        out_specs=(VMEM,) * 3,
        compiler_params=limit,
        name="strip",
    )(edge, own, low, high)
    from_left = ring(right, "gy", 1)
    from_right = ring(left, "gy", -1)

    def planes(*lead):
        return pltpu.VMEM(lead + (ROWS, LANES), jnp.float32)

    gram, mixes = pl.pallas_call(
        moments_kernel,
        out_shape=(shaped(8, 128), shaped(32, OWN_X, OWN_Y)),
        in_specs=[VMEM] * 5,
        out_specs=(VMEM,) * 2,
        scratch_shapes=[
            planes(PLANES),
            pltpu.VMEM((24, OWN_Y), jnp.float32),
            planes(11),
            planes(11),
            planes(11),
            planes(11),
            planes(11),
            planes(12),
            planes(2, 11),
            planes(2, 11),
            planes(4, 11),
            pltpu.VMEM((4, 11, OWN_X, OWN_Y), jnp.float32),
            planes(4, 4, 11),
            pltpu.VMEM((4, 53, OWN_X, OWN_Y), jnp.float32),
            planes(2, 16),
            pltpu.VMEM((5, 64, OWN_Y), jnp.float32),
            pltpu.VMEM((5, 128, OWN_Y), jnp.float32),
            pltpu.VMEM((10, 128, OWN_Y), jnp.float32),
            pltpu.VMEM((10, 256, OWN_Y), jnp.float32),
        ],
        compiler_params=limit,
        name="moments",
    )(edge, tall, high, from_left, from_right)
    gram = spread_sum(spread_sum(gram, "gx"), "gy")
    return pl.pallas_call(
        finish_kernel,
        out_shape=shaped(8, OWN_X, OWN_Y),
        in_specs=[VMEM] * 2,
        out_specs=VMEM,
        compiler_params=limit,
        name="finish",
    )(gram, mixes)


def solution(mesh):
    in_specs = (
        P(None, None, "gx", "gy"),
        P("gx", "gy"),
        P("gx", "gy"),
        P("gx", "gy"),
        P("gx", "gy"),
        P("gx", "gy"),
        P(None, "gx", "gy"),
    )
    out_specs = P(None, "gx", "gy")
    return jax.shard_map(body, mesh=mesh, in_specs=in_specs, out_specs=out_specs, check_vma=False)
```

```python
import jax
import jax.numpy as jnp
from jax import lax
from jax.experimental import pallas as pl
from jax.experimental.pallas import tpu as pltpu
from jax.sharding import PartitionSpec as P

MASS_TERM = 0.1
STRAIN_OFFSET = 0.01
PRECISE = lax.Precision.HIGHEST

ROWS = 16
LANES = 256
OWN_X = 8
OWN_Y = 128
LOW = 4
THICK, MASK, FRIC, OBS, PROBE = 22, 23, 24, 25, 26
PLANES = 34


def dot(left, right, dims=((1,), (0,))):
    return lax.dot_general(
        left, right, (dims, ((), ())), precision=PRECISE, preferred_element_type=jnp.float32
    )


def shift(plane, step, axis):
    size = plane.shape[axis]
    return pltpu.roll(plane, (-step) % size, axis)


def pack_kernel(vel, thick, logf, obs, mask, ground, probes, own, up, down, land, land_int, sems):
    moves = [
        (vel.at[0], own.at[pl.ds(0, 11)]),
        (vel.at[1], own.at[pl.ds(11, 11)]),
        (thick, own.at[THICK]),
        (probes, own.at[pl.ds(PROBE, 8)]),
        (logf, land.at[0]),
        (obs, land.at[1]),
        (mask, land_int.at[0]),
        (ground, land_int.at[1]),
    ]
    copies = [pltpu.make_async_copy(src, dst, sems.at[k]) for k, (src, dst) in enumerate(moves)]
    for copy in copies:
        copy.start()
    for copy in copies:
        copy.wait()
    m = land_int[0].astype(jnp.float32)
    own[MASK] = m
    own[FRIC] = m * land_int[1].astype(jnp.float32) * jnp.exp(land[0])
    own[OBS] = land[1] * m
    for k in range(PLANES):
        up[pl.ds(LOW * k, LOW), :] = own[k, OWN_X - LOW :, :]
        down[pl.ds(LOW * k, LOW), :] = own[k, :LOW, :]
        if k < 22:
            down[pl.ds(LOW * PLANES + k, 1), :] = own[k, LOW : LOW + 1, :]


def strip_kernel(edge, own, low, high, tall, left, right):
    keep_low, keep_high = edge[0:1, :], edge[1:2, :]
    for k in range(PLANES):
        tall[k, 0:OWN_X, :] = own[k]
        tall[k, OWN_X : OWN_X + LOW, :] = high[pl.ds(LOW * k, LOW), :] * keep_high
        tall[k, ROWS - LOW : ROWS, :] = low[pl.ds(LOW * k, LOW), :] * keep_low
    group = lax.broadcasted_iota(jnp.int32, (ROWS, OWN_Y), 1) // 8
    for b in range(3):
        first = last = jnp.zeros((ROWS, OWN_Y), jnp.float32)
        for g in range(min(16, PLANES - 16 * b)):
            moved = pltpu.roll(tall[16 * b + g], 8 * g, 1) if g else tall[16 * b]
            first = jnp.where(group == g, moved, first)
            last = jnp.where(group == (g + 15) % 16, moved, last)
        left[b] = first
        right[b] = last


def moments_kernel(
    edge, tall, high, from_left, from_right, gram, mixes,
    full, row12, mu, kx, kxm, ky, kym, kz, inv, ratio, resp, phi, gam, wts, basis,
    lhs8, rhs8, lhs16, rhs16,
):
    keep_high, keep_left, keep_right = edge[1:2, :], edge[2:3, :], edge[3:4, :]
    group = lax.broadcasted_iota(jnp.int32, (ROWS, OWN_Y), 1) // 8
    for b in range(3):
        above, below = from_right[b] * keep_right, from_left[b] * keep_left
        for g in range(min(16, PLANES - 16 * b)):
            k = 16 * b + g
            strips = jnp.where(group == g, above, jnp.where(group == (g + 15) % 16, below, 0.0))
            full[k, :, OWN_Y:] = pltpu.roll(strips, 128 - 8 * g, 1) if g else strips
            full[k, :, :OWN_Y] = tall[k]
    row12[...] = high[pl.ds(LOW * PLANES, 24), :] * keep_high

    m = full[MASK]
    icy = m > 0.5
    thick = jnp.where(icy, full[THICK], 1.0)
    steep = 10.0 / thick
    half_steep = 0.5 * steep
    steep2 = 0.5 * steep * steep
    mm_x = 0.5 * (m * shift(m, 1, 0))
    mm_y = 0.5 * (m * shift(m, 1, 1))
    fric = full[FRIC]
    base = MASS_TERM * m + (1.0 - m)
    last = lax.broadcasted_iota(jnp.int32, (ROWS, LANES), 0) == OWN_X + LOW - 1

    for l in range(11):
        grads = []
        for c in range(2):
            w = full[11 * c + l]
            beyond = jnp.concatenate(
                [row12[11 * c + l : 11 * c + l + 1, :], jnp.zeros((1, OWN_Y), jnp.float32)], axis=1
            )
            ahead = jnp.where(last, jnp.broadcast_to(beyond, (ROWS, LANES)), shift(w, 1, 0))
            gx = 0.5 * (ahead - shift(w, -1, 0))
            gy = 0.5 * (shift(w, 1, 1) - shift(w, -1, 1))
            gz = (full[11 * c + min(l + 1, 10)] - full[11 * c + max(l - 1, 0)]) * half_steep
            grads.append((gx, gy, gz))
        (ux, uy, uz), (vx, vy, vz) = grads
        cross = uy + vx
        e2 = ux * ux + vy * vy + ux * vy + 0.25 * (cross * cross + uz * uz + vz * vz) + STRAIN_OFFSET
        mu[l] = jnp.where(icy, 0.5 * jnp.exp(jnp.log(e2) * (-1.0 / 3.0)), 0.0)

    kz[0] = jnp.zeros((ROWS, LANES), jnp.float32)
    kz[11] = jnp.zeros((ROWS, LANES), jnp.float32)
    for l in range(11):
        here = mu[l]
        ex = (here + shift(here, 1, 0)) * mm_x
        ey = (here + shift(here, 1, 1)) * mm_y
        kx[l] = ex
        ky[l] = ey
        kxm[l] = shift(ex, -1, 0)
        kym[l] = shift(ey, -1, 1)
        if l < 10:
            kz[l + 1] = (here + mu[l + 1]) * steep2

    share, carry, top = [None] * 2, [None] * 2, [None] * 2
    for l in range(11):
        side_x, side_y = kx[l] + kxm[l], ky[l] + kym[l]
        rest = base + fric if l == 0 else base
        for c in range(2):
            excess = (4.0 * side_x + side_y if c == 0 else side_x + 4.0 * side_y) + rest
            if l > 0:
                excess = excess + kz[l] * share[c]
            recip = 1.0 / (excess + kz[l + 1])
            share[c] = excess * recip
            inv[c, l] = recip
            ratio[c, l] = kz[l + 1] * recip
            carry[c] = (fric * full[11 * c] if l == 0 else kz[l] * carry[c]) * recip
            resp[c, l] = carry[c]
            if l == 10:
                top[c] = recip
                resp[2 + c, 10] = recip
    for l in range(9, -1, -1):
        for c in range(2):
            step = ratio[c, l]
            carry[c] = resp[c, l] + step * carry[c]
            resp[c, l] = carry[c]
            top[c] = step * top[c]
            resp[2 + c, l] = top[c]

    def one_kind(kc, _):
        c = lax.rem(kc, 2)
        a = jnp.where(c == 0, 4.0, 1.0)
        b = 5.0 - a
        carry = [None] * 4
        n1 = [None] * 4
        for l in range(11):
            e = resp[kc, l]
            parts = [
                a * (kx[l] * shift(e, 1, 0)),
                a * (kxm[l] * shift(e, -1, 0)),
                b * (ky[l] * shift(e, 1, 1)),
                b * (kym[l] * shift(e, -1, 1)),
            ]
            scale = inv[c, l]
            for s in range(4):
                phi[s, l] = parts[s][:OWN_X, :OWN_Y]
                total = parts[s] if l == 0 else parts[s] + kz[l] * carry[s]
                carry[s] = total * scale
                gam[kc, s, l] = carry[s]
            for s in range(4):
                term = (e * parts[s])[:OWN_X, :OWN_Y]
                n1[s] = term if l == 0 else n1[s] + term
        for s in range(4):
            wts[kc, 1 + s] = n1[s]
        for l in range(9, -1, -1):
            step = ratio[c, l]
            for s in range(4):
                carry[s] = gam[kc, s, l] + step * carry[s]
                gam[kc, s, l] = carry[s]
        own = (slice(0, OWN_X), slice(0, OWN_Y))
        acc = [None] * 16
        for l in range(11):
            f = [phi[s, l] for s in range(4)]
            g = [gam[kc, s, l][own] for s in range(4)]
            for s in range(4):
                for t in range(s, 4):
                    term = f[s] * g[t]
                    acc[4 * s + t] = term if l == 0 else acc[4 * s + t] + term
        for s in range(4):
            for t in range(4):
                wts[kc, 5 + 4 * s + t] = acc[4 * min(s, t) + max(s, t)]
        for way in range(2):
            acc = [None] * 16
            for l in range(11):
                edge_k = kx[l][own] * a if way == 0 else ky[l][own] * b
                g = [gam[kc, s, l][own] * edge_k for s in range(4)]
                if way == 0:
                    h = [shift(gam[kc, s, l, :, :OWN_Y], 1, 0)[:OWN_X] for s in range(4)]
                else:
                    h = [shift(gam[kc, s, l, :OWN_X, :], 1, 1)[:, :OWN_Y] for s in range(4)]
                for s in range(4):
                    for t in range(4):
                        term = g[s] * h[t]
                        acc[4 * s + t] = term if l == 0 else acc[4 * s + t] + term
            for s in range(16):
                wts[kc, 21 + 16 * way + s] = acc[s]
        return 0

    lax.fori_loop(0, 4, one_kind, 0)
    own = (slice(0, OWN_X), slice(0, OWN_Y))
    for c in range(2):
        source = (fric * full[11 * c])[own]
        wts[c, 0] = source * resp[c, 0][own]
        wts[2 + c, 0] = resp[2 + c, 10][own]
    for k in range(53):
        wts[0, k] = wts[0, k] + wts[1, k]

    obs = full[OBS]

    def two_probes(step, _):
        for a in (2 * step, 2 * step + 1):
            p = full[PROBE + a]
            near = [shift(p, 1, 0), shift(p, -1, 0), shift(p, 1, 1), shift(p, -1, 1)]
            for c in range(2):
                basis[c, a] = obs * resp[c, 10] * p
                total = gam[c, 0, 10] * near[0]
                for s in range(1, 4):
                    total = total + gam[c, s, 10] * near[s]
                basis[c, 8 + a] = obs * total
        return 0

    lax.fori_loop(0, 4, two_probes, 0)

    def shifted(plane):
        mid = plane[:, :OWN_Y]
        yp = shift(plane, 1, 1)
        ym = shift(plane, -1, 1)[:, :OWN_Y]
        y2 = shift(yp[:OWN_X], 1, 1)[:, :OWN_Y]
        yp = yp[:, :OWN_Y]
        p00 = mid[:OWN_X]
        pxp, pxm, px2 = (shift(mid, d, 0)[:OWN_X] for d in (1, -1, 2))
        pyp, pxpyp, pxmyp = yp[:OWN_X], shift(yp, 1, 0)[:OWN_X], shift(yp, -1, 0)[:OWN_X]
        pym, pxpym = ym[:OWN_X], shift(ym, 1, 0)[:OWN_X]
        return p00, [pxp, pxm, pyp, pym], [px2, p00, pxpyp, pxpym], [pxpyp, pxmyp, y2, p00]

    def fill(kc, b, plane, many, lhs, rhs, first):
        p00, near, past_x, past_y = shifted(plane)
        here = pl.ds(b, OWN_X, stride=many)
        one = pl.ds(b, OWN_X, stride=2 * many)
        two = pl.ds(many + b, OWN_X, stride=2 * many)
        for t in range(4):
            second = wts[kc, 5 + 4 * t] * near[0]
            for s in range(1, 4):
                second = second + wts[kc, 5 + 4 * t + s] * near[s]
            third = wts[kc, 21 + 4 * t] * past_x[0] + wts[kc, 37 + 4 * t] * past_y[0]
            for s in range(1, 4):
                third = third + wts[kc, 21 + 4 * t + s] * past_x[s]
                third = third + wts[kc, 37 + 4 * t + s] * past_y[s]
            lhs[first + t, here, :] = near[t]
            rhs[first + t, one, :] = second
            rhs[first + t, two, :] = third
        lhs[first + 4, here, :] = p00
        rhs[first + 4, one, :] = wts[kc, 0] * p00
        side = wts[kc, 1] * near[0]
        for s in range(1, 4):
            side = side + wts[kc, 1 + s] * near[s]
        rhs[first + 4, two, :] = side
        return p00, near

    def side_by_side(ref, which, rows):
        return jnp.concatenate([ref[k, rows * x : rows * (x + 1)] for k in which for x in range(OWN_X)], axis=1)

    def fold(lhs, rhs, which, many):
        product = dot(side_by_side(lhs, which, many), side_by_side(rhs, which, 2 * many), ((1,), (1,)))
        return jnp.concatenate([product, jnp.zeros((many, 128 - 2 * many), jnp.float32)], axis=1)

    def fill_probe(step, _):
        for b in (4 * step, 4 * step + 1, 4 * step + 2, 4 * step + 3):
            fill(0, b, full[PROBE + b], 8, lhs8, rhs8, 0)
        return 0

    lax.fori_loop(0, 2, fill_probe, 0)

    weights = [(fric * full[11 * c])[own] for c in range(2)]

    def fill_basis(step, _):
        for b in (4 * step, 4 * step + 1, 4 * step + 2, 4 * step + 3):
            one = two = None
            for c in range(2):
                p00, near = fill(2 + c, b, basis[c, b], 16, lhs16, rhs16, 5 * c)
                here = resp[2 + c, 0, :OWN_X, :OWN_Y] * p00
                there = gam[2 + c, 0, 0, :OWN_X, :OWN_Y] * near[0]
                for s in range(1, 4):
                    there = there + gam[2 + c, s, 0, :OWN_X, :OWN_Y] * near[s]
                one = weights[c] * here if c == 0 else one + weights[c] * here
                two = weights[c] * there if c == 0 else two + weights[c] * there
            mixes[b] = one
            mixes[16 + b] = two
        return 0

    lax.fori_loop(0, 4, fill_basis, 0)

    ends8, sides8 = fold(lhs8, rhs8, (4,), 8), fold(lhs8, rhs8, (0, 1, 2, 3), 8)
    ends16, sides16 = fold(lhs16, rhs16, (4, 9), 16), fold(lhs16, rhs16, (0, 1, 2, 3, 5, 6, 7, 8), 16)

    def woven(ends, many):
        row, col = places(many, 128)
        other = pltpu.roll(ends, 128 - many, 1)
        line = jnp.sum(jnp.where(row == col, other, 0.0), axis=1, keepdims=True)
        return jnp.where(row <= col, ends, other), line

    square16, line16 = woven(ends16, 16)
    square8, line8 = woven(ends8, 8)
    _, col = places(16, 128)
    tall16 = jnp.where(col < 16, square16, pltpu.roll(sides16, 16, 1))
    _, col = places(8, 128)
    message = jnp.where(col < 48, tall16[:8], pltpu.roll(tall16[8:], 48, 1))
    message = jnp.where(col < 96, message, pltpu.roll(square8, 96, 1))
    message = jnp.where(col < 104, message, pltpu.roll(sides8, 104, 1))
    message = jnp.where(col < 120, message, line16[:8])
    message = jnp.where(col < 121, message, line16[8:])
    message = jnp.where(col < 122, message, line8)
    gram[...] = jnp.where(col < 123, message, 0.0)


def places(rows, cols):
    return lax.broadcasted_iota(jnp.int32, (rows, cols), 0), lax.broadcasted_iota(jnp.int32, (rows, cols), 1)


def turned(square):
    row, col = places(square.shape[0], square.shape[0])
    return dot(jnp.where(row == col, 1.0, 0.0), square, ((1,), (1,)))


def parted(packed, line):
    size = packed.shape[0]
    row, col = places(size, size)
    square = packed[:, :size]
    other = turned(square)
    half = packed[:, 2 * size : 3 * size]
    return (
        jnp.where(row <= col, square, other),
        jnp.where(row > col, square, jnp.where(row == col, line, other)),
        packed[:, size : 2 * size],
        half + turned(half),
    )


def krylov_solve(moments, sides):
    m0, m1, m2, m3 = moments
    low = m1 - m2
    square = jnp.concatenate(
        [jnp.concatenate([m0 - m1, low], axis=1), jnp.concatenate([low, m2 - m3], axis=1)], axis=0
    )
    row, col = places(16, 16)
    kept = jnp.where(row == col, square, 0.0)
    tall, wide = jnp.sum(kept, axis=1, keepdims=True), jnp.sum(kept, axis=0, keepdims=True)
    tall = jnp.where(tall > 0.0, lax.rsqrt(tall), 0.0)
    wide = jnp.where(wide > 0.0, lax.rsqrt(wide), 0.0)
    square = jnp.where((row == col) & (tall == 0.0), 1.0, square * tall * wide)
    system = jnp.concatenate([square, jnp.concatenate(sides, axis=0) * tall], axis=1)
    row, _ = places(*system.shape)
    for k in range(0, 16, 2):
        one, two = system[k : k + 1, :], system[k + 1 : k + 2, :]
        left = jnp.broadcast_to(system[:, k : k + 1], system.shape)
        right = jnp.broadcast_to(system[:, k + 1 : k + 2], system.shape)
        p, q = left[k : k + 1, :], right[k : k + 1, :]
        r, t = left[k + 1 : k + 2, :], right[k + 1 : k + 2, :]
        scale = 1.0 / (p * t - q * r)
        first = (t * one - q * two) * scale
        second = (p * two - r * one) * scale
        rest = system - left * first - right * second
        system = jnp.where(row == k, first, jnp.where(row == k + 1, second, rest))
    return system[:, 16:] * tall


def raised(coef):
    rows, cols = coef.shape
    tall = jnp.broadcast_to(coef[:, None, :], (rows, OWN_X, cols)).reshape(rows * OWN_X, cols)
    row, col = places(rows * OWN_X, cols)
    return jnp.where(row % OWN_X == col % OWN_X, tall, 0.0)


def finish_kernel(gram, mixes, out):
    tn = ((0,), (0,))
    row, col = places(8, 64)
    repeat = jnp.where(col // 8 == row, 1.0, 0.0)
    first = parted(gram[:, 96:120], gram[:, 122:123])
    wide = krylov_solve(first, [dot(first[0], repeat), dot(first[1], repeat)])
    row, col = places(64, 8)
    mix = dot(wide, jnp.where(row == 8 * col, 1.0, 0.0))
    adjoint = parted(
        jnp.concatenate([gram[:, 0:48], gram[:, 48:96]], axis=0),
        jnp.concatenate([gram[:, 120:121], gram[:, 121:122]], axis=0),
    )
    half = dot(mix, jnp.concatenate(adjoint, axis=1), tn)
    halves = [half[:, 16 * k : 16 * k + 16] for k in range(4)]
    second = [dot(part, mix) for part in halves]
    coef = krylov_solve(second, [dot(halves[0], wide), dot(halves[1], wide)])
    spread = raised(wide)
    flat = jnp.concatenate([dot(spread, mixes[16 * k : 16 * k + 16].reshape(128, OWN_Y), tn) for k in range(2)], axis=0)
    out[...] = dot(raised(coef), flat, tn).reshape(8, OWN_X, OWN_Y)


VMEM = pl.BlockSpec(memory_space=pltpu.VMEM)


def shaped(*dims):
    return jax.ShapeDtypeStruct(dims, jnp.float32)


def spread_sum(values, axis):
    count = lax.axis_size(axis)
    copies = jnp.broadcast_to(values, (count,) + values.shape)
    return jnp.sum(lax.all_to_all(copies, axis, 0, 0), axis=0)


def ring(values, axis, step):
    count = lax.axis_size(axis)
    return lax.ppermute(values, axis, [(i, (i + step) % count) for i in range(count)])


def body(velocity, thickness, log_friction, obs_weight, ice_mask, grounded, probes):
    at_x, at_y = lax.axis_index("gx"), lax.axis_index("gy")
    row = lax.broadcasted_iota(jnp.int32, (8, OWN_Y), 0)
    ends = [at_x, lax.axis_size("gx") - 1 - at_x, at_y, lax.axis_size("gy") - 1 - at_y]
    edge = jnp.ones((8, OWN_Y), jnp.float32)
    for k, end in enumerate(ends):
        edge = jnp.where((row == k) & (end == 0), 0.0, edge)
    limit = pltpu.CompilerParams(vmem_limit_bytes=48 * 1024 * 1024)
    args = (velocity, thickness, log_friction, obs_weight, ice_mask, grounded, probes)
    own, up, down = pl.pallas_call(
        pack_kernel,
        out_shape=(shaped(PLANES, OWN_X, OWN_Y), shaped(LOW * PLANES, OWN_Y), shaped(LOW * PLANES + 24, OWN_Y)),
        in_specs=[pl.BlockSpec(memory_space=pltpu.HBM)] * 7,
        out_specs=(VMEM,) * 3,
        scratch_shapes=[
            pltpu.VMEM((2, OWN_X, OWN_Y), jnp.float32),
            pltpu.VMEM((2, OWN_X, OWN_Y), jnp.int32),
            pltpu.SemaphoreType.DMA((8,)),
        ],
        compiler_params=limit,
        name="pack",
    )(*[pltpu.with_memory_space_constraint(value, pltpu.HBM) for value in args])
    low = ring(up, "gx", 1)
    high = ring(down, "gx", -1)
    tall, left, right = pl.pallas_call(
        strip_kernel,
        out_shape=(shaped(PLANES, ROWS, OWN_Y), shaped(3, ROWS, OWN_Y), shaped(3, ROWS, OWN_Y)),
        in_specs=[VMEM] * 4,
        out_specs=(VMEM,) * 3,
        compiler_params=limit,
        name="strip",
    )(edge, own, low, high)
    from_left = ring(right, "gy", 1)
    from_right = ring(left, "gy", -1)

    def planes(*lead):
        return pltpu.VMEM(lead + (ROWS, LANES), jnp.float32)

    gram, mixes = pl.pallas_call(
        moments_kernel,
        out_shape=(shaped(8, 128), shaped(32, OWN_X, OWN_Y)),
        in_specs=[VMEM] * 5,
        out_specs=(VMEM,) * 2,
        scratch_shapes=[
            planes(PLANES),
            pltpu.VMEM((24, OWN_Y), jnp.float32),
            planes(11),
            planes(11),
            planes(11),
            planes(11),
            planes(11),
            planes(12),
            planes(2, 11),
            planes(2, 11),
            planes(4, 11),
            pltpu.VMEM((4, 11, OWN_X, OWN_Y), jnp.float32),
            planes(4, 4, 11),
            pltpu.VMEM((4, 53, OWN_X, OWN_Y), jnp.float32),
            planes(2, 16),
            pltpu.VMEM((5, 64, OWN_Y), jnp.float32),
            pltpu.VMEM((5, 128, OWN_Y), jnp.float32),
            pltpu.VMEM((10, 128, OWN_Y), jnp.float32),
            pltpu.VMEM((10, 256, OWN_Y), jnp.float32),
        ],
        compiler_params=limit,
        name="moments",
    )(edge, tall, high, from_left, from_right)
    gram = spread_sum(spread_sum(gram, "gx"), "gy")
    return pl.pallas_call(
        finish_kernel,
        out_shape=shaped(8, OWN_X, OWN_Y),
        in_specs=[VMEM] * 2,
        out_specs=VMEM,
        compiler_params=limit,
        name="finish",
    )(gram, mixes)


def solution(mesh):
    in_specs = (
        P(None, None, "gx", "gy"),
        P("gx", "gy"),
        P("gx", "gy"),
        P("gx", "gy"),
        P("gx", "gy"),
        P("gx", "gy"),
        P(None, "gx", "gy"),
    )
    out_specs = P(None, "gx", "gy")
    return jax.shard_map(body, mesh=mesh, in_specs=in_specs, out_specs=out_specs, check_vma=False)
```

```python
import jax
import jax.numpy as jnp
from jax import lax
from jax.experimental import pallas as pl
from jax.experimental.pallas import tpu as pltpu
from jax.sharding import PartitionSpec as P

MASS_TERM = 0.1
STRAIN_OFFSET = 0.01
PRECISE = lax.Precision.HIGHEST

ROWS = 16
LANES = 256
OWN_X = 8
OWN_Y = 128
LOW = 4
THICK, MASK, FRIC, OBS, PROBE = 22, 23, 24, 25, 26
PLANES = 34


def dot(left, right, dims=((1,), (0,))):
    return lax.dot_general(
        left, right, (dims, ((), ())), precision=PRECISE, preferred_element_type=jnp.float32
    )


def shift(plane, step, axis):
    size = plane.shape[axis]
    return pltpu.roll(plane, (-step) % size, axis)


def pack_kernel(vel, thick, logf, obs, mask, ground, probes, own, up, down, land, land_int, sems):
    moves = [
        (vel.at[0], own.at[pl.ds(0, 11)]),
        (vel.at[1], own.at[pl.ds(11, 11)]),
        (thick, own.at[THICK]),
        (probes, own.at[pl.ds(PROBE, 8)]),
        (logf, land.at[0]),
        (obs, land.at[1]),
        (mask, land_int.at[0]),
        (ground, land_int.at[1]),
    ]
    copies = [pltpu.make_async_copy(src, dst, sems.at[k]) for k, (src, dst) in enumerate(moves)]
    for copy in copies:
        copy.start()
    for copy in copies:
        copy.wait()
    m = land_int[0].astype(jnp.float32)
    own[MASK] = m
    own[FRIC] = m * land_int[1].astype(jnp.float32) * jnp.exp(land[0])
    own[OBS] = land[1] * m
    for k in range(PLANES):
        up[pl.ds(LOW * k, LOW), :] = own[k, OWN_X - LOW :, :]
        down[pl.ds(LOW * k, LOW), :] = own[k, :LOW, :]
        if k < 22:
            down[pl.ds(LOW * PLANES + k, 1), :] = own[k, LOW : LOW + 1, :]


def strip_kernel(edge, own, low, high, tall, left, right):
    keep_low, keep_high = edge[0:1, :], edge[1:2, :]
    for k in range(PLANES):
        tall[k, 0:OWN_X, :] = own[k]
        tall[k, OWN_X : OWN_X + LOW, :] = high[pl.ds(LOW * k, LOW), :] * keep_high
        tall[k, ROWS - LOW : ROWS, :] = low[pl.ds(LOW * k, LOW), :] * keep_low
    group = lax.broadcasted_iota(jnp.int32, (ROWS, OWN_Y), 1) // 8
    for b in range(3):
        first = last = jnp.zeros((ROWS, OWN_Y), jnp.float32)
        for g in range(min(16, PLANES - 16 * b)):
            moved = pltpu.roll(tall[16 * b + g], 8 * g, 1) if g else tall[16 * b]
            first = jnp.where(group == g, moved, first)
            last = jnp.where(group == (g + 15) % 16, moved, last)
        left[b] = first
        right[b] = last


def moments_kernel(
    edge, tall, high, from_left, from_right, gram, mixes,
    full, row12, mu, kx, kxm, ky, kym, kz, inv, ratio, resp, phi, gam, wts, basis,
    lhs8, rhs8, lhs16, rhs16,
):
    keep_high, keep_left, keep_right = edge[1:2, :], edge[2:3, :], edge[3:4, :]
    group = lax.broadcasted_iota(jnp.int32, (ROWS, OWN_Y), 1) // 8
    for b in range(3):
        above, below = from_right[b] * keep_right, from_left[b] * keep_left
        for g in range(min(16, PLANES - 16 * b)):
            k = 16 * b + g
            strips = jnp.where(group == g, above, jnp.where(group == (g + 15) % 16, below, 0.0))
            full[k, :, OWN_Y:] = pltpu.roll(strips, 128 - 8 * g, 1) if g else strips
            full[k, :, :OWN_Y] = tall[k]
    row12[...] = high[pl.ds(LOW * PLANES, 24), :] * keep_high

    m = full[MASK]
    icy = m > 0.5
    thick = jnp.where(icy, full[THICK], 1.0)
    steep = 10.0 / thick
    half_steep = 0.5 * steep
    steep2 = 0.5 * steep * steep
    mm_x = 0.5 * (m * shift(m, 1, 0))
    mm_y = 0.5 * (m * shift(m, 1, 1))
    fric = full[FRIC]
    base = MASS_TERM * m + (1.0 - m)
    last = lax.broadcasted_iota(jnp.int32, (ROWS, LANES), 0) == OWN_X + LOW - 1

    for l in range(11):
        grads = []
        for c in range(2):
            w = full[11 * c + l]
            beyond = jnp.concatenate(
                [row12[11 * c + l : 11 * c + l + 1, :], jnp.zeros((1, OWN_Y), jnp.float32)], axis=1
            )
            ahead = jnp.where(last, jnp.broadcast_to(beyond, (ROWS, LANES)), shift(w, 1, 0))
            gx = 0.5 * (ahead - shift(w, -1, 0))
            gy = 0.5 * (shift(w, 1, 1) - shift(w, -1, 1))
            gz = (full[11 * c + min(l + 1, 10)] - full[11 * c + max(l - 1, 0)]) * half_steep
            grads.append((gx, gy, gz))
        (ux, uy, uz), (vx, vy, vz) = grads
        cross = uy + vx
        e2 = ux * ux + vy * vy + ux * vy + 0.25 * (cross * cross + uz * uz + vz * vz) + STRAIN_OFFSET
        mu[l] = jnp.where(icy, 0.5 * jnp.exp(jnp.log(e2) * (-1.0 / 3.0)), 0.0)

    kz[0] = jnp.zeros((ROWS, LANES), jnp.float32)
    kz[11] = jnp.zeros((ROWS, LANES), jnp.float32)
    for l in range(11):
        here = mu[l]
        ex = (here + shift(here, 1, 0)) * mm_x
        ey = (here + shift(here, 1, 1)) * mm_y
        kx[l] = ex
        ky[l] = ey
        kxm[l] = shift(ex, -1, 0)
        kym[l] = shift(ey, -1, 1)
        if l < 10:
            kz[l + 1] = (here + mu[l + 1]) * steep2

    share, carry, top = [None] * 2, [None] * 2, [None] * 2
    for l in range(11):
        side_x, side_y = kx[l] + kxm[l], ky[l] + kym[l]
        rest = base + fric if l == 0 else base
        for c in range(2):
            excess = (4.0 * side_x + side_y if c == 0 else side_x + 4.0 * side_y) + rest
            if l > 0:
                excess = excess + kz[l] * share[c]
            recip = 1.0 / (excess + kz[l + 1])
            share[c] = excess * recip
            inv[c, l] = recip
            ratio[c, l] = kz[l + 1] * recip
            carry[c] = (fric * full[11 * c] if l == 0 else kz[l] * carry[c]) * recip
            resp[c, l] = carry[c]
            if l == 10:
                top[c] = recip
                resp[2 + c, 10] = recip
    for l in range(9, -1, -1):
        for c in range(2):
            step = ratio[c, l]
            carry[c] = resp[c, l] + step * carry[c]
            resp[c, l] = carry[c]
            top[c] = step * top[c]
            resp[2 + c, l] = top[c]

    def one_kind(kc, _):
        c = lax.rem(kc, 2)
        a = jnp.where(c == 0, 4.0, 1.0)
        b = 5.0 - a
        carry = [None] * 4
        n1 = [None] * 4
        for l in range(11):
            e = resp[kc, l]
            parts = [
                a * (kx[l] * shift(e, 1, 0)),
                a * (kxm[l] * shift(e, -1, 0)),
                b * (ky[l] * shift(e, 1, 1)),
                b * (kym[l] * shift(e, -1, 1)),
            ]
            scale = inv[c, l]
            for s in range(4):
                phi[s, l] = parts[s][:OWN_X, :OWN_Y]
                total = parts[s] if l == 0 else parts[s] + kz[l] * carry[s]
                carry[s] = total * scale
                gam[kc, s, l] = carry[s]
            for s in range(4):
                term = (e * parts[s])[:OWN_X, :OWN_Y]
                n1[s] = term if l == 0 else n1[s] + term
        for s in range(4):
            wts[kc, 1 + s] = n1[s]
        for l in range(9, -1, -1):
            step = ratio[c, l]
            for s in range(4):
                carry[s] = gam[kc, s, l] + step * carry[s]
                gam[kc, s, l] = carry[s]
        own = (slice(0, OWN_X), slice(0, OWN_Y))
        acc = [None] * 16
        for l in range(11):
            f = [phi[s, l] for s in range(4)]
            g = [gam[kc, s, l][own] for s in range(4)]
            for s in range(4):
                for t in range(s, 4):
                    term = f[s] * g[t]
                    acc[4 * s + t] = term if l == 0 else acc[4 * s + t] + term
        for s in range(4):
            for t in range(4):
                wts[kc, 5 + 4 * s + t] = acc[4 * min(s, t) + max(s, t)]
        for way in range(2):
            acc = [None] * 16
            for l in range(11):
                edge_k = kx[l][own] * a if way == 0 else ky[l][own] * b
                g = [gam[kc, s, l][own] * edge_k for s in range(4)]
                if way == 0:
                    h = [shift(gam[kc, s, l, :, :OWN_Y], 1, 0)[:OWN_X] for s in range(4)]
                else:
                    h = [shift(gam[kc, s, l, :OWN_X, :], 1, 1)[:, :OWN_Y] for s in range(4)]
                for s in range(4):
                    for t in range(4):
                        term = g[s] * h[t]
                        acc[4 * s + t] = term if l == 0 else acc[4 * s + t] + term
            for s in range(16):
                wts[kc, 21 + 16 * way + s] = acc[s]
        return 0

    lax.fori_loop(0, 4, one_kind, 0)
    own = (slice(0, OWN_X), slice(0, OWN_Y))
    for c in range(2):
        source = (fric * full[11 * c])[own]
        wts[c, 0] = source * resp[c, 0][own]
        wts[2 + c, 0] = resp[2 + c, 10][own]
    for k in range(53):
        wts[0, k] = wts[0, k] + wts[1, k]

    obs = full[OBS]

    def four_probes(step, _):
        for a in [4 * step + k for k in range(4)]:
            p = full[PROBE + a]
            near = [shift(p, 1, 0), shift(p, -1, 0), shift(p, 1, 1), shift(p, -1, 1)]
            for c in range(2):
                basis[c, a] = obs * resp[c, 10] * p
                total = gam[c, 0, 10] * near[0]
                for s in range(1, 4):
                    total = total + gam[c, s, 10] * near[s]
                basis[c, 8 + a] = obs * total
        return 0

    lax.fori_loop(0, 2, four_probes, 0)

    def shifted(plane):
        mid = plane[:, :OWN_Y]
        yp = shift(plane, 1, 1)
        ym = shift(plane, -1, 1)[:, :OWN_Y]
        y2 = shift(yp[:OWN_X], 1, 1)[:, :OWN_Y]
        yp = yp[:, :OWN_Y]
        p00 = mid[:OWN_X]
        pxp, pxm, px2 = (shift(mid, d, 0)[:OWN_X] for d in (1, -1, 2))
        pyp, pxpyp, pxmyp = yp[:OWN_X], shift(yp, 1, 0)[:OWN_X], shift(yp, -1, 0)[:OWN_X]
        pym, pxpym = ym[:OWN_X], shift(ym, 1, 0)[:OWN_X]
        return p00, [pxp, pxm, pyp, pym], [px2, p00, pxpyp, pxpym], [pxpyp, pxmyp, y2, p00]

    def fill(kc, b, plane, many, lhs, rhs, first):
        p00, near, past_x, past_y = shifted(plane)
        here = pl.ds(b, OWN_X, stride=many)
        one = pl.ds(b, OWN_X, stride=2 * many)
        two = pl.ds(many + b, OWN_X, stride=2 * many)
        for t in range(4):
            second = wts[kc, 5 + 4 * t] * near[0]
            for s in range(1, 4):
                second = second + wts[kc, 5 + 4 * t + s] * near[s]
            third = wts[kc, 21 + 4 * t] * past_x[0] + wts[kc, 37 + 4 * t] * past_y[0]
            for s in range(1, 4):
                third = third + wts[kc, 21 + 4 * t + s] * past_x[s]
                third = third + wts[kc, 37 + 4 * t + s] * past_y[s]
            lhs[first + t, here, :] = near[t]
            rhs[first + t, one, :] = second
            rhs[first + t, two, :] = third
        lhs[first + 4, here, :] = p00
        rhs[first + 4, one, :] = wts[kc, 0] * p00
        side = wts[kc, 1] * near[0]
        for s in range(1, 4):
            side = side + wts[kc, 1 + s] * near[s]
        rhs[first + 4, two, :] = side
        return p00, near

    def side_by_side(ref, which, rows):
        return jnp.concatenate([ref[k, rows * x : rows * (x + 1)] for k in which for x in range(OWN_X)], axis=1)

    def fold(lhs, rhs, which, many):
        product = dot(side_by_side(lhs, which, many), side_by_side(rhs, which, 2 * many), ((1,), (1,)))
        return jnp.concatenate([product, jnp.zeros((many, 128 - 2 * many), jnp.float32)], axis=1)

    for b in range(8):
        fill(0, b, full[PROBE + b], 8, lhs8, rhs8, 0)

    weights = [(fric * full[11 * c])[own] for c in range(2)]

    def fill_basis(step, _):
        for b in [8 * step + k for k in range(8)]:
            one = two = None
            for c in range(2):
                p00, near = fill(2 + c, b, basis[c, b], 16, lhs16, rhs16, 5 * c)
                here = resp[2 + c, 0, :OWN_X, :OWN_Y] * p00
                there = gam[2 + c, 0, 0, :OWN_X, :OWN_Y] * near[0]
                for s in range(1, 4):
                    there = there + gam[2 + c, s, 0, :OWN_X, :OWN_Y] * near[s]
                one = weights[c] * here if c == 0 else one + weights[c] * here
                two = weights[c] * there if c == 0 else two + weights[c] * there
            mixes[b] = one
            mixes[16 + b] = two
        return 0

    lax.fori_loop(0, 2, fill_basis, 0)

    ends8, sides8 = fold(lhs8, rhs8, (4,), 8), fold(lhs8, rhs8, (0, 1, 2, 3), 8)
    ends16, sides16 = fold(lhs16, rhs16, (4, 9), 16), fold(lhs16, rhs16, (0, 1, 2, 3, 5, 6, 7, 8), 16)

    def woven(ends, many):
        row, col = places(many, 128)
        other = pltpu.roll(ends, 128 - many, 1)
        line = jnp.sum(jnp.where(row == col, other, 0.0), axis=1, keepdims=True)
        return jnp.where(row <= col, ends, other), line

    square16, line16 = woven(ends16, 16)
    square8, line8 = woven(ends8, 8)
    _, col = places(16, 128)
    tall16 = jnp.where(col < 16, square16, pltpu.roll(sides16, 16, 1))
    _, col = places(8, 128)
    message = jnp.where(col < 48, tall16[:8], pltpu.roll(tall16[8:], 48, 1))
    message = jnp.where(col < 96, message, pltpu.roll(square8, 96, 1))
    message = jnp.where(col < 104, message, pltpu.roll(sides8, 104, 1))
    message = jnp.where(col < 120, message, line16[:8])
    message = jnp.where(col < 121, message, line16[8:])
    message = jnp.where(col < 122, message, line8)
    gram[...] = jnp.where(col < 123, message, 0.0)


def places(rows, cols):
    return lax.broadcasted_iota(jnp.int32, (rows, cols), 0), lax.broadcasted_iota(jnp.int32, (rows, cols), 1)


def turned(square):
    row, col = places(square.shape[0], square.shape[0])
    return dot(jnp.where(row == col, 1.0, 0.0), square, ((1,), (1,)))


def parted(packed, line):
    size = packed.shape[0]
    row, col = places(size, size)
    square = packed[:, :size]
    other = turned(square)
    half = packed[:, 2 * size : 3 * size]
    return (
        jnp.where(row <= col, square, other),
        jnp.where(row > col, square, jnp.where(row == col, line, other)),
        packed[:, size : 2 * size],
        half + turned(half),
    )


def krylov_solve(moments, sides):
    m0, m1, m2, m3 = moments
    low = m1 - m2
    square = jnp.concatenate(
        [jnp.concatenate([m0 - m1, low], axis=1), jnp.concatenate([low, m2 - m3], axis=1)], axis=0
    )
    row, col = places(16, 16)
    kept = jnp.where(row == col, square, 0.0)
    tall, wide = jnp.sum(kept, axis=1, keepdims=True), jnp.sum(kept, axis=0, keepdims=True)
    tall = jnp.where(tall > 0.0, lax.rsqrt(tall), 0.0)
    wide = jnp.where(wide > 0.0, lax.rsqrt(wide), 0.0)
    square = jnp.where((row == col) & (tall == 0.0), 1.0, square * tall * wide)
    system = jnp.concatenate([square, jnp.concatenate(sides, axis=0) * tall], axis=1)
    row, _ = places(*system.shape)
    for k in range(0, 16, 2):
        one, two = system[k : k + 1, :], system[k + 1 : k + 2, :]
        left = jnp.broadcast_to(system[:, k : k + 1], system.shape)
        right = jnp.broadcast_to(system[:, k + 1 : k + 2], system.shape)
        p, q = left[k : k + 1, :], right[k : k + 1, :]
        r, t = left[k + 1 : k + 2, :], right[k + 1 : k + 2, :]
        scale = 1.0 / (p * t - q * r)
        first = (t * one - q * two) * scale
        second = (p * two - r * one) * scale
        rest = system - left * first - right * second
        system = jnp.where(row == k, first, jnp.where(row == k + 1, second, rest))
    return system[:, 16:] * tall


def raised(coef):
    rows, cols = coef.shape
    tall = jnp.broadcast_to(coef[:, None, :], (rows, OWN_X, cols)).reshape(rows * OWN_X, cols)
    row, col = places(rows * OWN_X, cols)
    return jnp.where(row % OWN_X == col % OWN_X, tall, 0.0)


def finish_kernel(gram, mixes, out):
    tn = ((0,), (0,))
    row, col = places(8, 64)
    repeat = jnp.where(col // 8 == row, 1.0, 0.0)
    first = parted(gram[:, 96:120], gram[:, 122:123])
    wide = krylov_solve(first, [dot(first[0], repeat), dot(first[1], repeat)])
    row, col = places(64, 8)
    mix = dot(wide, jnp.where(row == 8 * col, 1.0, 0.0))
    adjoint = parted(
        jnp.concatenate([gram[:, 0:48], gram[:, 48:96]], axis=0),
        jnp.concatenate([gram[:, 120:121], gram[:, 121:122]], axis=0),
    )
    half = dot(mix, jnp.concatenate(adjoint, axis=1), tn)
    halves = [half[:, 16 * k : 16 * k + 16] for k in range(4)]
    second = [dot(part, mix) for part in halves]
    coef = krylov_solve(second, [dot(halves[0], wide), dot(halves[1], wide)])
    spread = raised(wide)
    flat = jnp.concatenate([dot(spread, mixes[16 * k : 16 * k + 16].reshape(128, OWN_Y), tn) for k in range(2)], axis=0)
    out[...] = dot(raised(coef), flat, tn).reshape(8, OWN_X, OWN_Y)


VMEM = pl.BlockSpec(memory_space=pltpu.VMEM)


def shaped(*dims):
    return jax.ShapeDtypeStruct(dims, jnp.float32)


def spread_sum(values, axis):
    count = lax.axis_size(axis)
    copies = jnp.broadcast_to(values, (count,) + values.shape)
    return jnp.sum(lax.all_to_all(copies, axis, 0, 0), axis=0)


def ring(values, axis, step):
    count = lax.axis_size(axis)
    return lax.ppermute(values, axis, [(i, (i + step) % count) for i in range(count)])


def body(velocity, thickness, log_friction, obs_weight, ice_mask, grounded, probes):
    at_x, at_y = lax.axis_index("gx"), lax.axis_index("gy")
    row = lax.broadcasted_iota(jnp.int32, (8, OWN_Y), 0)
    ends = [at_x, lax.axis_size("gx") - 1 - at_x, at_y, lax.axis_size("gy") - 1 - at_y]
    edge = jnp.ones((8, OWN_Y), jnp.float32)
    for k, end in enumerate(ends):
        edge = jnp.where((row == k) & (end == 0), 0.0, edge)
    limit = pltpu.CompilerParams(vmem_limit_bytes=48 * 1024 * 1024)
    args = (velocity, thickness, log_friction, obs_weight, ice_mask, grounded, probes)
    own, up, down = pl.pallas_call(
        pack_kernel,
        out_shape=(shaped(PLANES, OWN_X, OWN_Y), shaped(LOW * PLANES, OWN_Y), shaped(LOW * PLANES + 24, OWN_Y)),
        in_specs=[pl.BlockSpec(memory_space=pltpu.HBM)] * 7,
        out_specs=(VMEM,) * 3,
        scratch_shapes=[
            pltpu.VMEM((2, OWN_X, OWN_Y), jnp.float32),
            pltpu.VMEM((2, OWN_X, OWN_Y), jnp.int32),
            pltpu.SemaphoreType.DMA((8,)),
        ],
        compiler_params=limit,
        name="pack",
    )(*[pltpu.with_memory_space_constraint(value, pltpu.HBM) for value in args])
    low = ring(up, "gx", 1)
    high = ring(down, "gx", -1)
    tall, left, right = pl.pallas_call(
        strip_kernel,
        out_shape=(shaped(PLANES, ROWS, OWN_Y), shaped(3, ROWS, OWN_Y), shaped(3, ROWS, OWN_Y)),
        in_specs=[VMEM] * 4,
        out_specs=(VMEM,) * 3,
        compiler_params=limit,
        name="strip",
    )(edge, own, low, high)
    from_left = ring(right, "gy", 1)
    from_right = ring(left, "gy", -1)

    def planes(*lead):
        return pltpu.VMEM(lead + (ROWS, LANES), jnp.float32)

    gram, mixes = pl.pallas_call(
        moments_kernel,
        out_shape=(shaped(8, 128), shaped(32, OWN_X, OWN_Y)),
        in_specs=[VMEM] * 5,
        out_specs=(VMEM,) * 2,
        scratch_shapes=[
            planes(PLANES),
            pltpu.VMEM((24, OWN_Y), jnp.float32),
            planes(11),
            planes(11),
            planes(11),
            planes(11),
            planes(11),
            planes(12),
            planes(2, 11),
            planes(2, 11),
            planes(4, 11),
            pltpu.VMEM((4, 11, OWN_X, OWN_Y), jnp.float32),
            planes(4, 4, 11),
            pltpu.VMEM((4, 53, OWN_X, OWN_Y), jnp.float32),
            planes(2, 16),
            pltpu.VMEM((5, 64, OWN_Y), jnp.float32),
            pltpu.VMEM((5, 128, OWN_Y), jnp.float32),
            pltpu.VMEM((10, 128, OWN_Y), jnp.float32),
            pltpu.VMEM((10, 256, OWN_Y), jnp.float32),
        ],
        compiler_params=limit,
        name="moments",
    )(edge, tall, high, from_left, from_right)
    gram = spread_sum(spread_sum(gram, "gx"), "gy")
    return pl.pallas_call(
        finish_kernel,
        out_shape=shaped(8, OWN_X, OWN_Y),
        in_specs=[VMEM] * 2,
        out_specs=VMEM,
        compiler_params=limit,
        name="finish",
    )(gram, mixes)


def solution(mesh):
    in_specs = (
        P(None, None, "gx", "gy"),
        P("gx", "gy"),
        P("gx", "gy"),
        P("gx", "gy"),
        P("gx", "gy"),
        P("gx", "gy"),
        P(None, "gx", "gy"),
    )
    out_specs = P(None, "gx", "gy")
    return jax.shard_map(body, mesh=mesh, in_specs=in_specs, out_specs=out_specs, check_vma=False)
```
